512 devices in a mesh: dp: 8 (over z_lo, core), feat: 64 (over y, x, z_hi).
Axes of the slice: x: 4, y: 8, z: 8 (z_hi: 2, z_lo: 4; z = z_hi * 4 + z_lo), core: 2. Of those that a mesh axis runs over, the one named last changes fastest.
Arguments:
- samples: bfloat16 [8192, 128], P('dp'), may hold values from -6 to 6
- projection: bfloat16 [128, 131072], P(None, ('dp', 'feat')), may hold values from -0.5 to 0.5
- phase_shift: bfloat16 [1, 131072], P(None, ('dp', 'feat')), may hold values from 0 to 6.28125
- solution: float32 [131072, 128], P(('dp', 'feat')), may hold values from -6 to 6
- residual: float32 [131072, 128], P(('dp', 'feat')), may hold values from -6 to 6
- direction: float32 [131072, 128], P(('dp', 'feat')), may hold values from -6 to 6
Outputs:
- solution_next: float32 [131072, 128], P(('dp', 'feat'))
- residual_next: float32 [131072, 128], P(('dp', 'feat'))
- direction_next: float32 [131072, 128], P(('dp', 'feat'))
The draws below stay inside these ranges and needn't reach their ends.
All inputs are finite; a program needn't handle non-finite values.
Results may differ from the reference program's by a relative error of at most 0.0015.
The reference program's roundings to bfloat16 on the way (of `feats`, `direction_low` and `row_sums`) count: a program that leaves them out, or rounds other values in their place, can miss the bound.
Values may be sent and summed in bfloat16 or wider, within the bound.
No kernel may reach another device: no remote copies, remote signals or barrier semaphores. Data moves between devices by JAX's collectives and lax.ppermute only.
A program may use at most 64 MiB of HBM per device.

```python
import math
import jax
import jax.numpy as jnp
from jax import lax

D = 128
FEATURES = 131072
TARGETS = 128
ROWS = 8192


def block_scale(own_key, shape, pieces, low, high):
    gain, own = 1.0, jax.random.fold_in(own_key, 6)
    for axis_at, parts in pieces:
        heights = jnp.exp(jax.random.uniform(jax.random.fold_in(own, axis_at), (parts,), jnp.float32, low / len(pieces), high / len(pieces)))
        gain = gain * jnp.repeat(heights, shape[axis_at] // parts).reshape([-1 if axis == axis_at else 1 for axis in range(len(shape))])
    return gain


def scatter_about(key, dims, scale, most, shards=(), held_as=jnp.bfloat16):
    gain = block_scale(key, dims, shards, -0.22, 0.18) if shards else 1.0
    values = jax.random.normal(key, dims, jnp.float32) * scale * gain
    return jnp.minimum(jnp.maximum(values, -most), most).astype(held_as)


def setup_inputs(seed: int = 0) -> dict:
    seeds = jax.random.split(jax.random.key(seed), 7)
    return {
        "samples": scatter_about(seeds[0], (ROWS, D), 1.0, 6.0, ((0, 8),)),
        "projection": scatter_about(seeds[1], (D, FEATURES), D ** -0.5, 0.5, ((1, 512),)),
        "phase_shift": jnp.clip(6.28125 * jax.random.uniform(seeds[2], (1, FEATURES), jnp.float32) ** block_scale(seeds[2], (1, FEATURES), ((1, 512),), -0.2, 0.2), 0.0, 6.28125).astype(jnp.bfloat16),
        "solution": scatter_about(seeds[3], (FEATURES, TARGETS), 1.0, 6.0, ((0, 512),), jnp.float32),
        "residual": scatter_about(seeds[4], (FEATURES, TARGETS), 1.0, 6.0, ((0, 512),), jnp.float32),
        "direction": scatter_about(seeds[5], (FEATURES, TARGETS), 1.0, 6.0, ((0, 512),), jnp.float32),
    }


penalty = 0.1
highest = lax.Precision.HIGHEST

def features(rows, proj_cols, shift_cols):
    phase = jnp.dot(rows.astype(jnp.float32), proj_cols.astype(jnp.float32), preferred_element_type=jnp.float32) + shift_cols.astype(jnp.float32)
    return (math.sqrt(2.0 / FEATURES) * jnp.cos(phase)).astype(jnp.bfloat16)

def symmetric(matrix):
    return 0.5 * (matrix + matrix.T)

def definite_solve(matrix, rhs):
    lower = jnp.linalg.cholesky(matrix)
    middle = lax.linalg.triangular_solve(lower, rhs, left_side=True, lower=True)
    return lax.linalg.triangular_solve(lower, middle, left_side=True, lower=True, transpose_a=True)

def reference(samples, projection, phase_shift, solution, residual, direction):
    block_size = math.gcd(FEATURES, 2048)
    block_count = FEATURES // block_size
    row_count = samples.shape[0]
    direction_low = direction.astype(jnp.bfloat16)
    proj_blocks = projection.reshape(D, block_count, block_size).transpose(1, 0, 2)
    shift_blocks = phase_shift.reshape(1, block_count, block_size).transpose(1, 0, 2)
    dir_blocks = direction_low.reshape(block_count, block_size, TARGETS)

    def accumulate(running, items):
        proj_piece, shift_piece, dir_piece = items
        feats = features(samples, proj_piece, shift_piece)
        return (running + jnp.dot(feats.astype(jnp.float32), dir_piece.astype(jnp.float32), preferred_element_type=jnp.float32), None)
    row_sums, unused = lax.scan(accumulate, jnp.zeros((row_count, TARGETS), jnp.float32), (proj_blocks, shift_blocks, dir_blocks))
    row_low = row_sums.astype(jnp.bfloat16)

    def back_project(items):
        proj_piece, shift_piece = items
        feats = features(samples, proj_piece, shift_piece)
        return lax.dot_general(feats.astype(jnp.float32), row_low.astype(jnp.float32), (((0,), (0,)), ((), ())), preferred_element_type=jnp.float32)
    applied = lax.map(back_project, (proj_blocks, shift_blocks)).reshape(FEATURES, TARGETS) + penalty * direction
    dir_gram = symmetric(jnp.dot(direction.T.astype(jnp.float32), applied.astype(jnp.float32), precision=highest, preferred_element_type=jnp.float32))
    res_gram = symmetric(jnp.dot(residual.T.astype(jnp.float32), residual.astype(jnp.float32), precision=highest, preferred_element_type=jnp.float32))
    step_coef = definite_solve(dir_gram, res_gram)
    solution_next = solution + jnp.dot(direction.astype(jnp.float32), step_coef.astype(jnp.float32), precision=highest, preferred_element_type=jnp.float32)
    residual_next = residual - jnp.dot(applied.astype(jnp.float32), step_coef.astype(jnp.float32), precision=highest, preferred_element_type=jnp.float32)
    res_gram_next = symmetric(jnp.dot(residual_next.T.astype(jnp.float32), residual_next.astype(jnp.float32), precision=highest, preferred_element_type=jnp.float32))
    mix_coef = definite_solve(res_gram, res_gram_next)
    direction_next = residual_next + jnp.dot(direction.astype(jnp.float32), mix_coef.astype(jnp.float32), precision=highest, preferred_element_type=jnp.float32)
    return (solution_next, residual_next, direction_next)
```

```python
import math

import jax
import jax.numpy as jnp
from jax import lax
from jax.experimental import pallas as pl
from jax.experimental.pallas import tpu as pltpu
from jax.sharding import Mesh, PartitionSpec as P

FEATURES = 131072
penalty = 0.1
highest = lax.Precision.HIGHEST
f32 = jnp.float32
bf16 = jnp.bfloat16

SINE = (6.283164044300415, -41.33714237083587, 81.34076887919463, -70.99343319457358)
SCALE = math.sqrt(2.0 / FEATURES)
ROUNDER = 12582912.0
PACK = 272
KDIM = 144
GRAM = 384

AXES = ("z2", "z1", "core", "y4", "y2", "y1", "x2", "x1", "zhi")
DP = ("z2", "z1", "core")
Z = ("z2", "z1")
ROW_NEAR = ("x2", "x1", "y1")
ROW_FAR = ("y4", "y2", "zhi")
GRAM_A = ("core", "x1", "y1")
GRAM_B = ("y4", "zhi", "x2")
GRAM_C = ("y2", "z2", "z1")


def vmem():
    return pl.BlockSpec(memory_space=pltpu.VMEM)


def call(kernel, outs, *args, scratch=(), flops=0, nbytes=0):
    return pl.pallas_call(
        kernel,
        out_shape=outs,
        in_specs=[vmem()] * len(args),
        out_specs=jax.tree.map(lambda _: vmem(), outs),
        scratch_shapes=list(scratch),
        compiler_params=pltpu.CompilerParams(vmem_limit_bytes=16 * 1024 * 1024),
        cost_estimate=pl.CostEstimate(flops=flops, bytes_accessed=nbytes, transcendentals=0),
    )(*args)


def struct(shape, dtype=f32):
    return jax.ShapeDtypeStruct(shape, dtype)


def pack_kernel(proj_ref, shift_ref, dir_ref, out_ref):
    shift = jnp.broadcast_to(shift_ref[...].astype(f32), (16, 256))
    first = lax.broadcasted_iota(jnp.int32, (16, 256), 0) == 0
    shift = jnp.where(first, shift, 0.0).astype(bf16)
    low = dir_ref[...].T.astype(bf16)
    for z in range(4):
        out_ref[z, 0:128, :] = proj_ref[...]
        out_ref[z, 128:144, :] = shift
        out_ref[z, 144:272, :] = low


def scaled_cos(phase):
    turns = phase * (1.0 / (2.0 * math.pi))
    turns = turns - ((turns + ROUNDER) - ROUNDER)
    w = 0.25 - jnp.abs(turns)
    z = w * w
    acc = SINE[3] * SCALE
    for c in (SINE[2], SINE[1], SINE[0]):
        acc = acc * z + c * SCALE
    return acc * w


def feature_steps(rows_t, pack_ref, feats_ref, acc):
    @pl.loop(0, 4)
    def _(s):
        piece = pack_ref.at[s]
        dir_t = piece[144:272, :]
        for r in range(4):
            cols = slice(r * 256, (r + 1) * 256)
            phase = lax.dot_general(
                piece[0:KDIM, :], rows_t[:, cols], (((0,), (0,)), ((), ())), preferred_element_type=f32
            )
            feats = scaled_cos(phase).astype(bf16)
            feats_ref[s, :, cols] = feats
            acc[:, cols] += jnp.dot(dir_t, feats, preferred_element_type=f32)


def own_features(samples_ref, pack_ref, feats_ref, acc, rows_t):
    rows_t[0:128, :] = samples_ref[...].T
    one = lax.broadcasted_iota(jnp.int32, (16, 1024), 0) == 0
    rows_t[128:144, :] = jnp.where(one, 1.0, 0.0).astype(bf16)
    acc[...] = jnp.zeros_like(acc)
    feature_steps(rows_t, pack_ref, feats_ref, acc)


def other_features(rows_t, acc_in, pack_ref, feats_ref, sums_ref, acc):
    acc[...] = acc_in[...]
    feature_steps(rows_t, pack_ref, feats_ref, acc)
    sums_ref[...] = acc[...].T


def sum_low_kernel(in_ref, out_ref):
    total = in_ref[0]
    for i in range(1, 8):
        total = total + in_ref[i]
    low = total.astype(bf16)
    for i in range(8):
        out_ref[i] = low


def sum_kernel(in_ref, out_ref):
    total = in_ref[0]
    for i in range(1, 8):
        total = total + in_ref[i]
    out_ref[...] = total


def sum_copies_kernel(in_ref, out_ref):
    total = in_ref[0]
    for i in range(1, 8):
        total = total + in_ref[i]
    for i in range(8):
        out_ref[i] = total


def back_kernel(feats_ref, low_ref, out_ref):
    for s in range(4):
        out_ref[s] = jnp.dot(feats_ref[s], low_ref[...], preferred_element_type=f32)


def fdot(a, b):
    return jnp.dot(a, b, precision=highest, preferred_element_type=f32)


def sym(m):
    return 0.5 * (m + m.T)


def places():
    n = 128
    return lax.broadcasted_iota(jnp.int32, (n, n), 0), lax.broadcasted_iota(jnp.int32, (n, n), 1)


def gram_kernel(parts_ref, dir_ref, res_ref, applied_ref, gram_ref):
    total = (parts_ref[0] + parts_ref[1]) + (parts_ref[2] + parts_ref[3])
    applied = total + penalty * dir_ref[...]
    applied_ref[...] = applied
    applied_t = applied.T
    dir_gram = sym(fdot(applied_t, dir_ref[...]))
    applied_gram = fdot(applied_t, applied)
    res_gram = sym(fdot(res_ref[...].T, res_ref[...]))
    at_row, at_col = places()
    diag = jnp.sum(jnp.where(at_row == at_col, applied_gram, 0.0), axis=1, keepdims=True)
    gram_ref[0:128, :] = jnp.where(at_col >= at_row, dir_gram, applied_gram)
    gram_ref[128:256, :] = fdot(applied_t, res_ref[...])
    gram_ref[256:384, :] = jnp.where(
        at_col >= at_row, res_gram, jnp.where(at_col == 0, diag, diag[0:1, 0:1])
    )


def lower_inverses(mats):
    n = 128
    lane = lax.broadcasted_iota(jnp.int32, (8, n), 1)
    sub = lax.broadcasted_iota(jnp.int32, (8, n), 0)
    lane1 = lane[0:1]
    tiles = [[m[8 * i : 8 * i + 8, :] for i in range(16)] for m in mats]
    for k in range(0, n, 2):
        home, at = divmod(k, 8)
        pair = (lane == k) | (lane == k + 1)
        for t in tiles:
            row_a = t[home][at : at + 1, :]
            row_b = t[home][at + 1 : at + 2, :]
            inv_a = 1.0 / row_a[:, k : k + 1]
            cross = row_b[:, k : k + 1]
            ratio = row_a[:, k + 1 : k + 2] * inv_a
            inv_b = 1.0 / (row_b[:, k + 1 : k + 2] - cross * ratio)
            low_a = jnp.where(lane1 == k, inv_a, row_a * inv_a)
            new_b = jnp.where(lane1 == k, 0.0, row_b) - cross * low_a
            low_b = jnp.where(lane1 == k + 1, inv_b, new_b * inv_b)
            low_a8 = jnp.broadcast_to(jnp.where(lane1 == k + 1, 0.0, low_a), (8, n))
            low_b8 = jnp.broadcast_to(low_b, (8, n))
            for i in range(home, 16):
                if i == home and at == 6:
                    t[i] = jnp.where(sub == at + 1, jnp.broadcast_to(new_b, (8, n)), t[i])
                    continue
                old = t[i]
                col_a = jnp.broadcast_to(old[:, k : k + 1], (8, n))
                col_b = jnp.broadcast_to(old[:, k + 1 : k + 2], (8, n)) - col_a * ratio
                new = jnp.where(pair, 0.0, old) - col_a * low_a8 - col_b * low_b8
                if i == home:
                    new = jnp.where(sub > at + 1, new, old)
                    new = jnp.where(sub == at + 1, jnp.broadcast_to(new_b, (8, n)), new)
                t[i] = new
    out = []
    at_row, at_col = places()
    for t in tiles:
        full = jnp.concatenate(t, axis=0)
        diag = jnp.sum(jnp.where(at_row == at_col, full, 0.0), axis=1, keepdims=True)
        inv = jnp.where(at_row > at_col, full, jnp.where(at_row == at_col, 1.0, 0.0))
        out.append((inv, 1.0 / diag))
    return out


def final_kernel(gram_ref, applied_ref, dir_ref, res_ref, sol_ref, sol_out, res_out, dir_out):
    at_row, at_col = places()
    first, cross, third = (gram_ref[128 * i : 128 * i + 128, :] for i in range(3))
    first_t, third_t = first.T, third.T
    dir_gram = jnp.where(at_col >= at_row, first, first_t)
    res_gram = jnp.where(at_col >= at_row, third, third_t)
    diag = jnp.where(at_row == 0, third[127:128, 1:2], third[:, 0:1])
    applied_gram = jnp.where(at_col < at_row, first, jnp.where(at_col == at_row, diag, first_t))
    (inv_d, scale_d), (inv_r, scale_r) = lower_inverses([dir_gram, res_gram])
    step = fdot(inv_d.T, scale_d * fdot(inv_d, res_gram))
    step_t = step.T
    sol_out[...] = sol_ref[...] + fdot(dir_ref[...], step)
    res_next = res_ref[...] - fdot(applied_ref[...], step)
    res_out[...] = res_next
    both = fdot(step_t, cross)
    gram_next = sym(res_gram - both - both.T + fdot(step_t, fdot(applied_gram, step)))
    mix = fdot(inv_r.T, scale_r * fdot(inv_r, gram_next))
    dir_out[...] = res_next + fdot(dir_ref[...], mix)


def swap_core(value):
    return lax.ppermute(value, "core", [(0, 1), (1, 0)])


def exchange(value, axes):
    return lax.all_to_all(value, axes, 0, 0)


def local(samples, projection, phase_shift, solution, residual, direction):
    pack = call(pack_kernel, struct((4, PACK, 256), bf16), projection, phase_shift, direction)
    own = exchange(pack, Z)
    other = swap_core(own)
    work = 2 * 2 * 1024 * 1024 * 128
    own_feats, acc, rows_t = call(
        own_features,
        [struct((4, 256, 1024), bf16), struct((128, 1024)), struct((KDIM, 1024), bf16)],
        samples,
        own,
        flops=10 * work,
    )
    other_feats, sums = call(
        other_features,
        [struct((4, 256, 1024), bf16), struct((1024, 128))],
        rows_t,
        acc,
        other,
        scratch=[pltpu.VMEM((128, 1024), f32)],
        flops=10 * work,
    )
    near = exchange(sums.reshape(8, 128, 128), ROW_NEAR)
    near = call(sum_kernel, struct((128, 128)), near)
    far = exchange(near.reshape(8, 16, 128), ROW_FAR)
    far = call(sum_low_kernel, struct((8, 16, 128), bf16), far)
    low = exchange(far, ROW_FAR).reshape(128, 128)
    low = exchange(jnp.broadcast_to(low[None], (8, 128, 128)), ROW_NEAR).reshape(1024, 128)
    theirs = call(back_kernel, struct((4, 256, 128)), other_feats, low, flops=work // 2)
    theirs = swap_core(theirs)
    mine = call(back_kernel, struct((4, 256, 128)), own_feats, low, flops=work // 2)
    parts = exchange(mine + theirs, Z)
    applied, gram = call(
        gram_kernel, [struct((256, 128)), struct((GRAM, 128))], parts, direction, residual
    )
    chunk = GRAM // 8
    piece = exchange(gram.reshape(8, chunk, 128), GRAM_A)
    for axes in (GRAM_B, GRAM_C, GRAM_A):
        piece = call(sum_copies_kernel, struct((8, chunk, 128)), piece)
        piece = exchange(piece, axes)
    return call(
        final_kernel,
        [struct((256, 128))] * 3,
        piece.reshape(GRAM, 128),
        applied,
        direction,
        residual,
        solution,
    )


def solution(mesh):
    fine = Mesh(mesh.devices.reshape((2,) * 9), AXES)
    rows, cols, state = P(DP, None), P(None, AXES), P(AXES, None)
    return jax.shard_map(
        local,
        mesh=fine,
        in_specs=(rows, cols, cols, state, state, state),
        out_specs=(state, state, state),
        check_vma=False,
    )
```

```python
import math

import jax
import jax.numpy as jnp
from jax import lax
from jax.experimental import pallas as pl
from jax.experimental.pallas import tpu as pltpu
from jax.sharding import Mesh, PartitionSpec as P

FEATURES = 131072
penalty = 0.1
highest = lax.Precision.HIGHEST
f32 = jnp.float32
bf16 = jnp.bfloat16

SINE = (6.283164044300415, -41.33714237083587, 81.34076887919463, -70.99343319457358)
SCALE = math.sqrt(2.0 / FEATURES)
ROUNDER = 12582912.0
PACK = 272
GRAM = 384

AXES = ("z2", "z1", "core", "y4", "y2", "y1", "x2", "x1", "zhi")
DP = ("z2", "z1", "core")
RING_X = ("x2", "x1")
RING_Y = ("y4", "y2", "y1")
RING_Z = ("zhi", "z2", "z1")
CHIP_X = ("x2", "x1", "core")


def vmem():
    return pl.BlockSpec(memory_space=pltpu.VMEM)


def call(kernel, outs, *args, scratch=(), flops=0, nbytes=0):
    return pl.pallas_call(
        kernel,
        out_shape=outs,
        in_specs=[vmem()] * len(args),
        out_specs=jax.tree.map(lambda _: vmem(), outs),
        scratch_shapes=list(scratch),
        compiler_params=pltpu.CompilerParams(vmem_limit_bytes=16 * 1024 * 1024),
        cost_estimate=pl.CostEstimate(flops=flops, bytes_accessed=nbytes, transcendentals=0),
    )(*args)


def struct(shape, dtype=f32):
    return jax.ShapeDtypeStruct(shape, dtype)


def pack_kernel(proj_in, shift_in, dir_in, out_ref, proj_ref, shift_ref, dir_ref, sems):
    copies = [
        pltpu.make_async_copy(src, dst, sems.at[i])
        for i, (src, dst) in enumerate(
            ((dir_in, dir_ref), (proj_in, proj_ref), (shift_in, shift_ref))
        )
    ]
    for c in copies:
        c.start()
    for c in copies:
        c.wait()
    proj_t = proj_ref[...].astype(f32).T.astype(bf16)
    out_ref[0:128, 0:128] = proj_t[0:128]
    out_ref[0:128, 128:256] = proj_t[128:256]
    out_ref[128:144, :] = jnp.broadcast_to(shift_ref[...].astype(f32), (16, 256)).astype(bf16)
    out_ref[144:272, :] = dir_ref[...].T.astype(bf16)


def scaled_cos(phase):
    turns = phase * (1.0 / (2.0 * math.pi))
    turns = turns - ((turns + ROUNDER) - ROUNDER)
    w = 0.25 - jnp.abs(turns)
    z = w * w
    acc = SINE[3] * SCALE
    for c in (SINE[2], SINE[1], SINE[0]):
        acc = acc * z + c * SCALE
    return acc * w


def feature_step(rows_t, piece, feats_ref, acc):
    proj_t = jnp.concatenate([piece[0:128, 0:128], piece[0:128, 128:256]], axis=0)
    shift = piece[128:144, :].astype(f32).T[:, 0:1]
    dir_t = piece[144:272, :]
    for r in range(4):
        cols = slice(r * 256, (r + 1) * 256)
        phase = jnp.dot(proj_t, rows_t[:, cols], preferred_element_type=f32)
        for i in range(0, 256, 32):
            strip = phase[i : i + 32] + shift[i : i + 32]
            feats_ref[i : i + 32, cols] = scaled_cos(strip).astype(bf16)
        acc[:, cols] += jnp.dot(dir_t, feats_ref[:, cols], preferred_element_type=f32)


def own_features(samples_ref, pack_ref, feats_ref, acc, rows_t):
    rows_t[...] = samples_ref[...].T
    acc[...] = jnp.zeros_like(acc)
    feature_step(rows_t, pack_ref, feats_ref.at[0], acc)


def more_features(rows_t, acc_in, *refs):
    packs, feats_ref, acc = refs[:-2], refs[-2], refs[-1]
    acc[...] = acc_in[...]
    for s, p in enumerate(packs):
        feature_step(rows_t, p, feats_ref.at[s], acc)


def stack_kernel(a_ref, b_ref, c_ref, after_ref, out_ref):
    for s, r in enumerate((a_ref, b_ref, c_ref)):
        out_ref[s] = r[...]


def last_features(rows_t, acc_in, pack_ref, feats_ref, sums_ref, acc):
    acc[...] = acc_in[...]

    @pl.loop(0, 3)
    def _(s):
        feature_step(rows_t, pack_ref.at[s], feats_ref.at[s], acc)

    sums_ref[...] = acc[...].T


def total_of(in_ref):
    total = in_ref[0]
    for i in range(1, in_ref.shape[0]):
        total = total + in_ref[i]
    return total


def sum_kernel(in_ref, out_ref):
    out_ref[...] = total_of(in_ref)


def sum_copies_kernel(in_ref, out_ref):
    total = total_of(in_ref)
    for i in range(8):
        out_ref[i] = total


def low_copies_kernel(a_ref, b_ref, out_ref):
    low = (a_ref[...] + b_ref[...]).astype(bf16)
    for i in range(8):
        out_ref[i] = low


def add_kernel(a_ref, b_ref, *outs):
    for i in range(4):
        outs[i][...] = a_ref[i] + b_ref[i]


def back_kernel(near_ref, far_ref, low_ref, out_ref):
    out_ref[0] = jnp.dot(near_ref[0], low_ref[...], preferred_element_type=f32)
    for s in range(3):
        out_ref[s + 1] = jnp.dot(far_ref[s], low_ref[...], preferred_element_type=f32)


def fdot(a, b):
    return jnp.dot(a, b, precision=highest, preferred_element_type=f32)


def sym(m):
    return 0.5 * (m + m.T)


def places():
    n = 128
    return lax.broadcasted_iota(jnp.int32, (n, n), 0), lax.broadcasted_iota(jnp.int32, (n, n), 1)


def gram_kernel(p0, p1, p2, p3, dir_ref, res_ref, applied_ref, gram_ref):
    total = (p0[...] + p1[...]) + (p2[...] + p3[...])
    applied = total + penalty * dir_ref[...]
    applied_ref[...] = applied
    applied_t = applied.T
    dir_gram = sym(fdot(applied_t, dir_ref[...]))
    applied_gram = fdot(applied_t, applied)
    res_gram = sym(fdot(res_ref[...].T, res_ref[...]))
    at_row, at_col = places()
    diag = jnp.sum(jnp.where(at_row == at_col, applied_gram, 0.0), axis=1, keepdims=True)
    gram_ref[0:128, :] = jnp.where(at_col >= at_row, dir_gram, applied_gram)
    gram_ref[128:256, :] = fdot(applied_t, res_ref[...])
    gram_ref[256:384, :] = jnp.where(
        at_col >= at_row, res_gram, jnp.where(at_col == 0, diag, diag[0:1, 0:1])
    )


def inverse_factors(mats):
    n, w = 128, 8
    lane = lax.broadcasted_iota(jnp.int32, (w, n), 1)
    sub = lax.broadcasted_iota(jnp.int32, (w, n), 0)

    def row(tile, i):
        return jnp.broadcast_to(tile[i : i + 1, :], (w, n))

    def col(tile, i):
        return jnp.broadcast_to(tile[:, i : i + 1], (w, n))

    tiles = [[m[w * i : w * i + w, :] for i in range(n // w)] for m in mats]
    outs = [([], []) for _ in mats]
    for h in range(n // w):
        k = w * h
        inside = (lane >= k) & (lane < k + w)
        for t, (ms, ns) in zip(tiles, outs):
            home = t[h]
            rows = [row(home, i) for i in range(w)]
            p = {(i, j): col(rows[i], k + j) for i in range(w) for j in range(i + 1)}
            r = [jnp.where(inside, jnp.where(lane == k + i, 1.0, 0.0), rows[i]) for i in range(w)]
            inv, low = [], {}
            for j in range(w):
                inv.append(1.0 / p[j, j])
                for i in range(j + 1, w):
                    low[i, j] = p[i, j] * inv[j]
                for i in range(j + 1, w):
                    for m in range(j + 1, i + 1):
                        p[i, m] = p[i, m] - low[i, j] * p[m, j]
                    r[i] = r[i] - low[i, j] * r[j]
            x = [None] * w
            for j in reversed(range(w)):
                x[j] = r[j] * inv[j]
                for i in range(j + 1, w):
                    x[j] = x[j] - low[i, j] * x[i]
            for i in range(h + 1, n // w):
                old = t[i]
                new = jnp.where(inside, 0.0, old)
                for j in range(w):
                    new = new - col(old, k + j) * x[j]
                t[i] = new
            whole = x[0]
            for j in range(1, w):
                whole = jnp.where(sub == j, x[j], whole)
            ms.append(jnp.where(lane < k, home, jnp.where(lane == sub + k, 1.0, 0.0)))
            ns.append(jnp.where(lane < k + w, whole, 0.0))
    return [(jnp.concatenate(ms, axis=0), jnp.concatenate(ns, axis=0)) for ms, ns in outs]


def final_kernel(gram_ref, applied_ref, dir_ref, res_ref, sol_ref, sol_out, res_out, dir_out):
    at_row, at_col = places()
    first, cross, third = (gram_ref[128 * i : 128 * i + 128, :] for i in range(3))
    first_t, third_t = first.T, third.T
    dir_gram = jnp.where(at_col >= at_row, first, first_t)
    res_gram = jnp.where(at_col >= at_row, third, third_t)
    diag = jnp.where(at_row == 0, third[127:128, 1:2], third[:, 0:1])
    applied_gram = jnp.where(at_col < at_row, first, jnp.where(at_col == at_row, diag, first_t))
    (m_d, n_d), (m_r, n_r) = inverse_factors([dir_gram, res_gram])
    step = fdot(m_d.T, fdot(n_d, res_gram))
    step_t = step.T
    sol_out[...] = sol_ref[...] + fdot(dir_ref[...], step)
    res_next = res_ref[...] - fdot(applied_ref[...], step)
    res_out[...] = res_next
    both = fdot(step_t, cross)
    gram_next = sym(res_gram - both - both.T + fdot(step_t, fdot(applied_gram, step)))
    mix = fdot(m_r.T, fdot(n_r, gram_next))
    dir_out[...] = res_next + fdot(dir_ref[...], mix)


def swap(value, axes, s):
    n = 2 ** len(axes)
    return lax.ppermute(value, axes, [(i, i ^ s) for i in range(n)])


def exchange(value, axes):
    return lax.all_to_all(value, axes, 0, 0)


def local(samples, projection, phase_shift, solution, residual, direction):
    z_lo = ("z2", "z1")
    core = ("core",)
    pack = pl.pallas_call(
        pack_kernel,
        out_shape=struct((PACK, 256), bf16),
        in_specs=[pl.BlockSpec(memory_space=pltpu.HBM)] * 3,
        out_specs=vmem(),
        scratch_shapes=[
            pltpu.VMEM((128, 256), bf16),
            pltpu.VMEM((1, 256), bf16),
            pltpu.VMEM((256, 128), f32),
            pltpu.SemaphoreType.DMA((3,)),
        ],
        compiler_params=pltpu.CompilerParams(vmem_limit_bytes=63000000),
    )(projection, phase_shift, direction)
    along = [swap(pack, z_lo, s) for s in (1, 2, 3)]
    across = swap(pack, core, 1)
    work = 2 * 2 * 1024 * 256 * 128 * 10

    def feats_of(n):
        return struct((n, 256, 1024), bf16)

    acc_of = struct((128, 1024))
    own, acc, rows_t = call(
        own_features, [feats_of(1), acc_of, struct((128, 1024), bf16)], samples, pack, flops=work
    )
    other, acc = call(more_features, [feats_of(1), acc_of], rows_t, acc, across, flops=work)
    stacked = pl.pallas_call(
        stack_kernel,
        out_shape=struct((3, PACK, 256), bf16),
        in_specs=[vmem()] * 3 + [pl.BlockSpec(memory_space=pl.ANY)],
        out_specs=vmem(),
        compiler_params=pltpu.CompilerParams(vmem_limit_bytes=16 * 1024 * 1024),
    )(*along, acc)
    across_far = swap(stacked, core, 1)
    own_far, acc = call(more_features, [feats_of(3), acc_of], rows_t, acc, *along, flops=3 * work)
    other_far, sums = call(
        last_features,
        [feats_of(3), struct((1024, 128))],
        rows_t,
        acc,
        across_far,
        scratch=[pltpu.VMEM((128, 1024), f32)],
        flops=3 * work,
    )
    by_x = call(sum_kernel, struct((256, 128)), exchange(sums.reshape(4, 256, 128), RING_X))
    by_y = call(sum_kernel, struct((32, 128)), exchange(by_x.reshape(8, 32, 128), RING_Y))
    low = call(low_copies_kernel, struct((8, 32, 128), bf16), by_y, swap(by_y, ("zhi",), 1))
    low = exchange(low, RING_Y).reshape(256, 128)
    low = exchange(jnp.broadcast_to(low[None], (4, 256, 128)), RING_X).reshape(1024, 128)
    theirs = call(back_kernel, struct((4, 256, 128)), other, other_far, low, flops=work // 5)
    theirs = swap(theirs, core, 1)
    mine = call(back_kernel, struct((4, 256, 128)), own, own_far, low, flops=work // 5)
    parts = call(add_kernel, [struct((256, 128))] * 4, mine, theirs)
    parts = [parts[0]] + [swap(parts[s], z_lo, s) for s in (1, 2, 3)]
    applied, gram = call(
        gram_kernel, [struct((256, 128)), struct((GRAM, 128))], *parts, direction, residual
    )
    chunk = GRAM // 8
    piece = exchange(gram.reshape(8, chunk, 128), CHIP_X)
    for axes in (RING_Y, RING_Z, CHIP_X):
        piece = call(sum_copies_kernel, struct((8, chunk, 128)), piece)
        piece = exchange(piece, axes)
    return call(
        final_kernel,
        [struct((256, 128))] * 3,
        piece.reshape(GRAM, 128),
        applied,
        direction,
        residual,
        solution,
    )


def solution(mesh):
    fine = Mesh(mesh.devices.reshape((2,) * 9), AXES)
    rows, cols, state = P(DP, None), P(None, AXES), P(AXES, None)
    return jax.shard_map(
        local,
        mesh=fine,
        in_specs=(rows, cols, cols, state, state, state),
        out_specs=(state, state, state),
        check_vma=False,
    )
```

```python
import functools
import math

import jax
import jax.numpy as jnp
from jax import lax
from jax.experimental import pallas as pl
from jax.experimental.pallas import tpu as pltpu
from jax.sharding import Mesh, PartitionSpec as P

FEATURES = 131072
penalty = 0.1
highest = lax.Precision.HIGHEST
f32 = jnp.float32
bf16 = jnp.bfloat16

SINE = (6.283164044300415, -41.33714237083587, 81.34076887919463, -70.99343319457358)
SCALE = math.sqrt(2.0 / FEATURES)
ROUNDER = 12582912.0
PACK = 272
GRAM = 384

AXES = ("z2", "z1", "core", "y4", "y2", "y1", "x2", "x1", "zhi")
DP = ("z2", "z1", "core")
RING_X = ("x2", "x1")
RING_Y = ("y4", "y2", "y1")
RING_Z = ("zhi", "z2", "z1")
CHIP_X = ("x2", "x1", "core")


def vmem():
    return pl.BlockSpec(memory_space=pltpu.VMEM)


def call(kernel, outs, *args, scratch=(), flops=0, ids=(), after=None):
    args = (*ids, *args)
    specs = [pl.BlockSpec(memory_space=pltpu.SMEM)] * len(ids) + [vmem()] * (len(args) - len(ids))
    if after is not None:
        args, specs = (*args, after), [*specs, pl.BlockSpec(memory_space=pl.ANY)]
    return pl.pallas_call(
        kernel,
        out_shape=outs,
        in_specs=specs,
        out_specs=jax.tree.map(lambda _: vmem(), outs),
        scratch_shapes=list(scratch),
        compiler_params=pltpu.CompilerParams(vmem_limit_bytes=16 * 1024 * 1024),
        cost_estimate=pl.CostEstimate(flops=flops, bytes_accessed=0, transcendentals=0),
    )(*args)


def struct(shape, dtype=f32):
    return jax.ShapeDtypeStruct(shape, dtype)


def pack_kernel(proj_in, shift_in, dir_in, out_ref, proj_ref, shift_ref, dir_ref, sems):
    copies = [
        pltpu.make_async_copy(src, dst, sems.at[i])
        for i, (src, dst) in enumerate(
            ((dir_in, dir_ref), (proj_in, proj_ref), (shift_in, shift_ref))
        )
    ]
    for c in copies:
        c.start()
    for c in copies:
        c.wait()
    proj_t = proj_ref[...].astype(f32).T.astype(bf16)
    out_ref[0:128, 0:128] = proj_t[0:128]
    out_ref[0:128, 128:256] = proj_t[128:256]
    out_ref[128:144, :] = jnp.broadcast_to(shift_ref[...].astype(f32), (16, 256)).astype(bf16)
    out_ref[144:272, :] = dir_ref[...].T.astype(bf16)


def scaled_cos(phase):
    turns = phase * (1.0 / (2.0 * math.pi))
    turns = turns - ((turns + ROUNDER) - ROUNDER)
    w = 0.25 - jnp.abs(turns)
    z = w * w
    acc = SINE[3] * SCALE
    for c in (SINE[2], SINE[1], SINE[0]):
        acc = acc * z + c * SCALE
    return acc * w


def feature_step(rows_t, piece, feats_ref, acc, quarters, base):
    proj_t = jnp.concatenate([piece[0:128, 0:128], piece[0:128, 128:256]], axis=0)
    shift = piece[128:144, :].astype(f32).T[:, 0:1]
    dir_t = piece[144:272, :]
    for q in quarters:
        rows = slice(q * 256, (q + 1) * 256)
        cols = slice((q - base) * 256, (q - base + 1) * 256)
        phase = jnp.dot(proj_t, rows_t[:, rows], preferred_element_type=f32)
        for i in range(0, 256, 32):
            strip = phase[i : i + 32] + shift[i : i + 32]
            feats_ref[i : i + 32, cols] = scaled_cos(strip).astype(bf16)
        acc[:, cols] += jnp.dot(dir_t, feats_ref[:, cols], preferred_element_type=f32)


def first_features(ids_ref, samples_ref, pack_ref, feats_ref, acc, rows_t):
    for q in range(4):
        start = pl.multiple_of((ids_ref[0] ^ q) * 256, 256)
        rows_t[:, q * 256 : (q + 1) * 256] = samples_ref[pl.ds(start, 256), :].T
    acc[...] = jnp.zeros_like(acc)
    feature_step(rows_t, pack_ref, feats_ref, acc, range(4), 0)


def their_near_features(rows_t, acc_in, p1, after_ref, feats_ref, acc):
    acc[...] = acc_in[...]
    feature_step(rows_t, p1, feats_ref, acc, range(4), 0)


def their_far_features(rows_t, acc_in, p2, p3, feats_ref, sums_ref, acc):
    acc[...] = acc_in[...]
    for s, p in enumerate((p2, p3)):
        feature_step(rows_t, p, feats_ref.at[s], acc, range(4), 0)
    sums_ref[...] = acc[...].T


def own_quarter(q, rows_t, acc_in, p1, p2, p3, *refs):
    feats_ref, sums_ref, acc = refs[-3:]
    acc[...] = acc_in[:, q * 256 : (q + 1) * 256]
    for s, p in enumerate((p1, p2, p3)):
        feature_step(rows_t, p, feats_ref.at[s], acc, (q,), q)
    total = acc[...].T
    if len(refs) == 5:
        total = total + refs[0][q * 256 : (q + 1) * 256, :]
    sums_ref[...] = total


def add_quarter(q, own_ref, other_ref, out_ref):
    out_ref[...] = own_ref[...] + other_ref[q * 256 : (q + 1) * 256, :]


def four_sum(a, b, c, d, out_ref):
    total = (a[...] + b[...]) + (c[...] + d[...])
    for y in range(8):
        for z in range(2):
            out_ref[2 * y + z] = total[32 * y : 32 * y + 32]


def total_of(in_ref):
    total = in_ref[0]
    for i in range(1, in_ref.shape[0]):
        total = total + in_ref[i]
    return total


def sum_copies_kernel(in_ref, out_ref):
    total = total_of(in_ref)
    for i in range(8):
        out_ref[i] = total


def low_copies_kernel(in_ref, out_ref):
    low = total_of(in_ref).astype(bf16)
    for i in range(32):
        out_ref[i] = low


def own_back(ids_ref, first_ref, f0, f1, f2, f3, low_ref, *outs):
    quarters = (f0, f1, f2, f3)
    for s in range(4):
        total = jnp.zeros((256, 128), f32)
        for q in range(4):
            feats = first_ref[:, q * 256 : (q + 1) * 256] if s == 0 else quarters[q][s - 1]
            total += jnp.dot(feats, low_ref[ids_ref[0] ^ q], preferred_element_type=f32)
        outs[s][...] = total


def their_back(ids_ref, first_ref, near_ref, far_ref, low_ref, a0, a1, a2, a3, *outs):
    for s, part in enumerate((a0, a1, a2, a3)):
        total = part[...]
        for q in range(4):
            cols = slice(q * 256, (q + 1) * 256)
            feats = (first_ref, near_ref, far_ref.at[0], far_ref.at[1])[s][:, cols]
            total += jnp.dot(feats, low_ref[ids_ref[0] ^ q], preferred_element_type=f32)
        outs[s][...] = total


def fdot(a, b):
    return jnp.dot(a, b, precision=highest, preferred_element_type=f32)


def sym(m):
    return 0.5 * (m + m.T)


def places():
    n = 128
    return lax.broadcasted_iota(jnp.int32, (n, n), 0), lax.broadcasted_iota(jnp.int32, (n, n), 1)


def gram_kernel(p0, p1, p2, p3, dir_ref, res_ref, applied_ref, gram_ref):
    total = (p0[...] + p1[...]) + (p2[...] + p3[...])
    applied = total + penalty * dir_ref[...]
    applied_ref[...] = applied
    applied_t = applied.T
    dir_gram = sym(fdot(applied_t, dir_ref[...]))
    applied_gram = fdot(applied_t, applied)
    res_gram = sym(fdot(res_ref[...].T, res_ref[...]))
    at_row, at_col = places()
    diag = jnp.sum(jnp.where(at_row == at_col, applied_gram, 0.0), axis=1, keepdims=True)
    gram_ref[0:128, :] = jnp.where(at_col >= at_row, dir_gram, applied_gram)
    gram_ref[128:256, :] = fdot(applied_t, res_ref[...])
    gram_ref[256:384, :] = jnp.where(
        at_col >= at_row, res_gram, jnp.where(at_col == 0, diag, diag[0:1, 0:1])
    )


def inverse_factors(mats):
    n, w = 128, 8
    lane = lax.broadcasted_iota(jnp.int32, (w, n), 1)
    sub = lax.broadcasted_iota(jnp.int32, (w, n), 0)

    def row(tile, i):
        return jnp.broadcast_to(tile[i : i + 1, :], (w, n))

    def col(tile, i):
        return jnp.broadcast_to(tile[:, i : i + 1], (w, n))

    tiles = [[m[w * i : w * i + w, :] for i in range(n // w)] for m in mats]
    outs = [([], []) for _ in mats]
    for h in range(n // w):
        k = w * h
        inside = (lane >= k) & (lane < k + w)
        for t, (ms, ns) in zip(tiles, outs):
            home = t[h]
            rows = [row(home, i) for i in range(w)]
            p = {(i, j): col(rows[i], k + j) for i in range(w) for j in range(i + 1)}
            r = [jnp.where(inside, jnp.where(lane == k + i, 1.0, 0.0), rows[i]) for i in range(w)]
            inv, low = [], {}
            for j in range(w):
                inv.append(1.0 / p[j, j])
                for i in range(j + 1, w):
                    low[i, j] = p[i, j] * inv[j]
                for i in range(j + 1, w):
                    for m in range(j + 1, i + 1):
                        p[i, m] = p[i, m] - low[i, j] * p[m, j]
                    r[i] = r[i] - low[i, j] * r[j]
            x = [None] * w
            for j in reversed(range(w)):
                x[j] = r[j] * inv[j]
                for i in range(j + 1, w):
                    x[j] = x[j] - low[i, j] * x[i]
            whole = x[0]
            for j in range(1, w):
                whole = jnp.where(sub == j, x[j], whole)
            if h + 1 < n // w:
                right = jnp.where(lane >= k + w, home, 0.0)
                change = lax.dot_general(
                    right, whole, (((0,), (0,)), ((), ())), precision=highest, preferred_element_type=f32
                )
                for i in range(h + 2, n // w):
                    t[i] = jnp.where(inside, 0.0, t[i]) - change[w * i : w * i + w]
                old = t[h + 1]
                new = jnp.where(inside, 0.0, old)
                for j in range(w):
                    new = new - col(old, k + j) * x[j]
                t[h + 1] = new
            ms.append(jnp.where(lane < k, home, jnp.where(lane == sub + k, 1.0, 0.0)))
            ns.append(jnp.where(lane < k + w, whole, 0.0))
    return [(jnp.concatenate(ms, axis=0), jnp.concatenate(ns, axis=0)) for ms, ns in outs]


def final_kernel(gram_ref, applied_ref, dir_ref, res_ref, sol_ref, sol_out, res_out, dir_out):
    at_row, at_col = places()
    first, cross, third = (gram_ref[128 * i : 128 * i + 128, :] for i in range(3))
    first_t, third_t = first.T, third.T
    dir_gram = jnp.where(at_col >= at_row, first, first_t)
    res_gram = jnp.where(at_col >= at_row, third, third_t)
    diag = jnp.where(at_row == 0, third[127:128, 1:2], third[:, 0:1])
    applied_gram = jnp.where(at_col < at_row, first, jnp.where(at_col == at_row, diag, first_t))
    (m_d, n_d), (m_r, n_r) = inverse_factors([dir_gram, res_gram])
    step = fdot(m_d.T, fdot(n_d, res_gram))
    step_t = step.T
    sol_out[...] = sol_ref[...] + fdot(dir_ref[...], step)
    res_next = res_ref[...] - fdot(applied_ref[...], step)
    res_out[...] = res_next
    both = fdot(step_t, cross)
    gram_next = sym(res_gram - both - both.T + fdot(step_t, fdot(applied_gram, step)))
    mix = fdot(m_r.T, fdot(n_r, gram_next))
    dir_out[...] = res_next + fdot(dir_ref[...], mix)


def swap(value, axes, s):
    n = 2 ** len(axes)
    return lax.ppermute(value, axes, [(i, i ^ s) for i in range(n)])


def exchange(value, axes):
    return lax.all_to_all(value, axes, 0, 0)


def local(samples, projection, phase_shift, solution, residual, direction):
    z_lo = ("z2", "z1")
    core = ("core",)
    pack = pl.pallas_call(
        pack_kernel,
        out_shape=struct((PACK, 256), bf16),
        in_specs=[pl.BlockSpec(memory_space=pltpu.HBM)] * 3,
        out_specs=vmem(),
        scratch_shapes=[
            pltpu.VMEM((128, 256), bf16),
            pltpu.VMEM((1, 256), bf16),
            pltpu.VMEM((256, 128), f32),
            pltpu.SemaphoreType.DMA((3,)),
        ],
        compiler_params=pltpu.CompilerParams(vmem_limit_bytes=63000000),
    )(projection, phase_shift, direction)
    along = [swap(pack, z_lo, s) for s in (1, 2, 3)]
    other_samples = swap(samples, core, 1)
    ids = (lax.axis_index(RING_X).astype(jnp.int32).reshape(1),)
    work = 2 * 2 * 1024 * 256 * 128 * 10
    acc_of, rows_of = struct((128, 1024)), struct((128, 1024), bf16)
    feats_of = struct((256, 1024), bf16)
    part, low_part = struct((256, 128)), struct((3, 256, 256), bf16)
    firsts = [feats_of, acc_of, rows_of]
    own_first, own_acc, own_rows = call(first_features, firsts, samples, pack, flops=work, ids=ids)
    their_first, their_acc, their_rows = call(
        first_features, firsts, other_samples, pack, flops=work, ids=ids
    )
    their_near, their_acc = call(
        their_near_features,
        [feats_of, acc_of],
        their_rows,
        their_acc,
        along[0],
        after=own_acc,
        flops=work,
    )
    their_far, their_sums = call(
        their_far_features,
        [struct((2, 256, 1024), bf16), struct((1024, 128))],
        their_rows,
        their_acc,
        *along[1:],
        scratch=[pltpu.VMEM((128, 1024), f32)],
        flops=2 * work,
    )
    from_other = swap(their_sums, core, 1)
    own_rest, sums, last = [None] * 4, [None] * 4, their_sums
    for q in (2, 1, 3, 0):
        own_rest[q], sums[q] = call(
            functools.partial(own_quarter, q),
            [low_part, part],
            own_rows,
            own_acc,
            *along,
            *(() if q == 2 else (from_other,)),
            after=last,
            scratch=[pltpu.VMEM((128, 256), f32)],
            flops=3 * work // 4,
        )
        last = sums[q]
        if q == 2:
            last = sums[q] = call(functools.partial(add_quarter, q), part, sums[q], from_other)
        if q:
            sums[q] = swap(sums[q], RING_X, q)
    pieces = exchange(call(four_sum, struct((16, 32, 128)), *sums), RING_Y + ("zhi",))
    low = call(low_copies_kernel, struct((32, 32, 128), bf16), pieces)
    low = exchange(low, RING_X + RING_Y).reshape(4, 256, 128)
    other_low = swap(low, core, 1)
    parts = call(own_back, [part] * 4, own_first, *own_rest, low, flops=work // 5, ids=ids)
    parts = call(
        their_back, [part] * 4, their_first, their_near, their_far, other_low, *parts, flops=work // 5, ids=ids
    )
    parts = [parts[0]] + [swap(parts[s], z_lo, s) for s in (1, 2, 3)]
    applied, gram = call(
        gram_kernel, [struct((256, 128)), struct((GRAM, 128))], *parts, direction, residual
    )
    chunk = GRAM // 8
    piece = exchange(gram.reshape(8, chunk, 128), CHIP_X)
    for axes in (RING_Y, RING_Z, CHIP_X):
        piece = call(sum_copies_kernel, struct((8, chunk, 128)), piece)
        piece = exchange(piece, axes)
    return call(
        final_kernel,
        [struct((256, 128))] * 3,
        piece.reshape(GRAM, 128),
        applied,
        direction,
        residual,
        solution,
    )


def solution(mesh):
    fine = Mesh(mesh.devices.reshape((2,) * 9), AXES)
    rows, cols, state = P(DP, None), P(None, AXES), P(AXES, None)
    return jax.shard_map(
        local,
        mesh=fine,
        in_specs=(rows, cols, cols, state, state, state),
        out_specs=(state, state, state),
        check_vma=False,
    )
```

```python
import functools
import math

import jax
import jax.numpy as jnp
from jax import lax
from jax.experimental import pallas as pl
from jax.experimental.pallas import tpu as pltpu
from jax.sharding import Mesh, PartitionSpec as P

FEATURES = 131072
penalty = 0.1
highest = lax.Precision.HIGHEST
f32 = jnp.float32
bf16 = jnp.bfloat16

SINE = (6.283164044300415, -41.33714237083587, 81.34076887919463, -70.99343319457358)
SCALE = math.sqrt(2.0 / FEATURES)
ROUNDER = 12582912.0
PACK = 272
GRAM = 512

AXES = ("z2", "z1", "core", "y4", "y2", "y1", "x2", "x1", "zhi")
DP = ("z2", "z1", "core")
RING_X = ("x2", "x1")
RING_Y = ("y4", "y2", "y1")
RING_Z = ("zhi", "z2", "z1")


def vmem():
    return pl.BlockSpec(memory_space=pltpu.VMEM)


def call(kernel, outs, *args, scratch=(), flops=0, ids=(), after=None):
    args = (*ids, *args)
    specs = [pl.BlockSpec(memory_space=pltpu.SMEM)] * len(ids) + [vmem()] * (len(args) - len(ids))
    if after is not None:
        args, specs = (*args, after), [*specs, pl.BlockSpec(memory_space=pl.ANY)]
    return pl.pallas_call(
        kernel,
        out_shape=outs,
        in_specs=specs,
        out_specs=jax.tree.map(lambda _: vmem(), outs),
        scratch_shapes=list(scratch),
        compiler_params=pltpu.CompilerParams(vmem_limit_bytes=16 * 1024 * 1024),
        cost_estimate=pl.CostEstimate(flops=flops, bytes_accessed=0, transcendentals=0),
    )(*args)


def struct(shape, dtype=f32):
    return jax.ShapeDtypeStruct(shape, dtype)


def pack_kernel(proj_in, shift_in, dir_in, out_ref, proj_ref, shift_ref, dir_ref, sems):
    copies = [
        pltpu.make_async_copy(src, dst, sems.at[i])
        for i, (src, dst) in enumerate(
            ((dir_in, dir_ref), (proj_in, proj_ref), (shift_in, shift_ref))
        )
    ]
    for c in copies:
        c.start()
    for c in copies:
        c.wait()
    proj_t = proj_ref[...].astype(f32).T.astype(bf16)
    out_ref[0:128, 0:128] = proj_t[0:128]
    out_ref[0:128, 128:256] = proj_t[128:256]
    out_ref[128:144, :] = jnp.broadcast_to(shift_ref[...].astype(f32), (16, 256)).astype(bf16)
    out_ref[144:272, :] = dir_ref[...].T.astype(bf16)


def scaled_cos(phase):
    turns = phase * (1.0 / (2.0 * math.pi))
    turns = turns - ((turns + ROUNDER) - ROUNDER)
    w = 0.25 - jnp.abs(turns)
    z = w * w
    acc = SINE[3] * SCALE
    for c in (SINE[2], SINE[1], SINE[0]):
        acc = acc * z + c * SCALE
    return acc * w


def feature_step(rows_t, piece, feats_ref, acc, quarters, base):
    proj_t = jnp.concatenate([piece[0:128, 0:128], piece[0:128, 128:256]], axis=0)
    shift = piece[128:144, :].astype(f32).T[:, 0:1]
    dir_t = piece[144:272, :]
    for q in quarters:
        rows = slice(q * 256, (q + 1) * 256)
        cols = slice((q - base) * 256, (q - base + 1) * 256)
        phase = jnp.dot(proj_t, rows_t[:, rows], preferred_element_type=f32)
        for i in range(0, 256, 32):
            strip = phase[i : i + 32] + shift[i : i + 32]
            feats_ref[i : i + 32, cols] = scaled_cos(strip).astype(bf16)
        acc[:, cols] += jnp.dot(dir_t, feats_ref[:, cols], preferred_element_type=f32)


def first_features(ids_ref, samples_ref, pack_ref, feats_ref, acc, rows_t):
    for q in range(4):
        start = pl.multiple_of((ids_ref[0] ^ q) * 256, 256)
        rows_t[:, q * 256 : (q + 1) * 256] = samples_ref[pl.ds(start, 256), :].T
    acc[...] = jnp.zeros_like(acc)
    feature_step(rows_t, pack_ref, feats_ref, acc, range(4), 0)


def their_near_features(rows_t, acc_in, p1, after_ref, feats_ref, acc):
    acc[...] = acc_in[...]
    feature_step(rows_t, p1, feats_ref, acc, range(4), 0)


def their_far_features(rows_t, acc_in, p2, p3, feats_ref, sums_ref, acc):
    acc[...] = acc_in[...]
    for s, p in enumerate((p2, p3)):
        feature_step(rows_t, p, feats_ref.at[s], acc, range(4), 0)
    sums_ref[...] = acc[...].T


def own_quarter(q, rows_t, acc_in, p1, p2, p3, *refs):
    feats_ref, sums_ref, acc = refs[-3:]
    acc[...] = acc_in[:, q * 256 : (q + 1) * 256]
    for s, p in enumerate((p1, p2, p3)):
        feature_step(rows_t, p, feats_ref.at[s], acc, (q,), q)
    total = acc[...].T
    if len(refs) == 5:
        total = total + refs[0][q * 256 : (q + 1) * 256, :]
    sums_ref[...] = total


def add_quarter(q, own_ref, other_ref, out_ref):
    out_ref[...] = own_ref[...] + other_ref[q * 256 : (q + 1) * 256, :]


def four_sum(a, b, c, d, out_ref):
    total = (a[...] + b[...]) + (c[...] + d[...])
    for y in range(8):
        for z in range(2):
            out_ref[2 * y + z] = total[32 * y : 32 * y + 32]


def total_of(in_ref):
    total = in_ref[0]
    for i in range(1, in_ref.shape[0]):
        total = total + in_ref[i]
    return total


def sum_copies_kernel(in_ref, out_ref):
    total = total_of(in_ref)
    for i in range(out_ref.shape[0]):
        out_ref[i] = total


def low_copies_kernel(in_ref, out_ref):
    low = total_of(in_ref).astype(bf16)
    for i in range(32):
        out_ref[i] = low


def own_back(ids_ref, first_ref, f0, f1, f2, f3, low_ref, *outs):
    quarters = (f0, f1, f2, f3)
    for s in range(4):
        total = jnp.zeros((256, 128), f32)
        for q in range(4):
            feats = first_ref[:, q * 256 : (q + 1) * 256] if s == 0 else quarters[q][s - 1]
            total += jnp.dot(feats, low_ref[ids_ref[0] ^ q], preferred_element_type=f32)
        outs[s][...] = total


def their_far_back(ids_ref, far_ref, low_ref, a2, a3, *outs):
    for s, part in enumerate((a2, a3)):
        total = part[...]
        for q in range(4):
            feats = far_ref[s, :, q * 256 : (q + 1) * 256]
            total += jnp.dot(feats, low_ref[ids_ref[0] ^ q], preferred_element_type=f32)
        outs[s][...] = total


def their_near_back(ids_ref, first_ref, near_ref, low_ref, a0, a1, after_ref, *outs):
    for s, (ref, part) in enumerate(((first_ref, a0), (near_ref, a1))):
        total = part[...]
        for q in range(4):
            feats = ref[:, q * 256 : (q + 1) * 256]
            total += jnp.dot(feats, low_ref[ids_ref[0] ^ q], preferred_element_type=f32)
        outs[s][...] = total


def fdot(a, b):
    return jnp.dot(a, b, precision=highest, preferred_element_type=f32)


def sym(m):
    return 0.5 * (m + m.T)


def two_sum(a, b, out_ref):
    out_ref[...] = a[...] + b[...]


def gram_kernel(far, own, near, dir_ref, res_ref, applied_ref, gram_ref):
    total = far[...] + (own[...] + near[...])
    applied = total + penalty * dir_ref[...]
    applied_ref[...] = applied
    applied_t = applied.T
    grams = (
        fdot(applied_t, dir_ref[...]),
        fdot(applied_t, res_ref[...]),
        fdot(applied_t, applied),
        fdot(res_ref[...].T, res_ref[...]),
    )
    for i, g in enumerate(grams):
        gram_ref[128 * i : 128 * i + 128, :] = g


def inverse_factors(mats):
    n, w = 128, 8
    lane = lax.broadcasted_iota(jnp.int32, (w, n), 1)
    sub = lax.broadcasted_iota(jnp.int32, (w, n), 0)

    def row(tile, i):
        return jnp.broadcast_to(tile[i : i + 1, :], (w, n))

    def col(tile, i):
        return jnp.broadcast_to(tile[:, i : i + 1], (w, n))

    tiles = [[m[w * i : w * i + w, :] for i in range(n // w)] for m in mats]
    outs = [([], []) for _ in mats]
    for h in range(n // w):
        k = w * h
        inside = (lane >= k) & (lane < k + w)
        for t, (ms, ns) in zip(tiles, outs):
            home = t[h]
            rows = [row(home, i) for i in range(w)]
            p = {(i, j): col(rows[i], k + j) for i in range(w) for j in range(i + 1)}
            r = [jnp.where(inside, jnp.where(lane == k + i, 1.0, 0.0), rows[i]) for i in range(w)]
            inv, low = [], {}
            for j in range(w):
                inv.append(1.0 / p[j, j])
                for i in range(j + 1, w):
                    low[i, j] = p[i, j] * inv[j]
                for i in range(j + 1, w):
                    for m in range(j + 1, i + 1):
                        p[i, m] = p[i, m] - low[i, j] * p[m, j]
                    r[i] = r[i] - low[i, j] * r[j]
            x = [None] * w
            for j in reversed(range(w)):
                x[j] = r[j] * inv[j]
                for i in range(j + 1, w):
                    x[j] = x[j] - low[i, j] * x[i]
            whole = x[0]
            for j in range(1, w):
                whole = jnp.where(sub == j, x[j], whole)
            if h + 1 < n // w:
                right = jnp.where(lane >= k + w, home, 0.0)
                change = lax.dot_general(
                    right, whole, (((0,), (0,)), ((), ())), precision=highest, preferred_element_type=f32
                )
                for i in range(h + 2, n // w):
                    t[i] = jnp.where(inside, 0.0, t[i]) - change[w * i : w * i + w]
                old = t[h + 1]
                new = jnp.where(inside, 0.0, old)
                for j in range(w):
                    new = new - col(old, k + j) * x[j]
                t[h + 1] = new
            ms.append(jnp.where(lane < k, home, jnp.where(lane == sub + k, 1.0, 0.0)))
            ns.append(jnp.where(lane < k + w, whole, 0.0))
    return [(jnp.concatenate(ms, axis=0), jnp.concatenate(ns, axis=0)) for ms, ns in outs]


def final_kernel(gram_ref, applied_ref, dir_ref, res_ref, sol_ref, sol_out, res_out, dir_out):
    dir_gram = sym(gram_ref[0:128, :])
    cross = gram_ref[128:256, :]
    applied_gram = gram_ref[256:384, :]
    res_gram = sym(gram_ref[384:512, :])
    (m_d, n_d), (m_r, n_r) = inverse_factors([dir_gram, res_gram])
    step = fdot(m_d.T, fdot(n_d, res_gram))
    step_t = step.T
    sol_out[...] = sol_ref[...] + fdot(dir_ref[...], step)
    res_next = res_ref[...] - fdot(applied_ref[...], step)
    res_out[...] = res_next
    both = fdot(step_t, cross)
    gram_next = sym(res_gram - both - both.T + fdot(step_t, fdot(applied_gram, step)))
    mix = fdot(m_r.T, fdot(n_r, gram_next))
    dir_out[...] = res_next + fdot(dir_ref[...], mix)


def swap(value, axes, s):
    n = 2 ** len(axes)
    return lax.ppermute(value, axes, [(i, i ^ s) for i in range(n)])


def exchange(value, axes):
    return lax.all_to_all(value, axes, 0, 0)


def local(samples, projection, phase_shift, solution, residual, direction):
    z_lo = ("z2", "z1")
    core = ("core",)
    pack = pl.pallas_call(
        pack_kernel,
        out_shape=struct((PACK, 256), bf16),
        in_specs=[pl.BlockSpec(memory_space=pltpu.HBM)] * 3,
        out_specs=vmem(),
        scratch_shapes=[
            pltpu.VMEM((128, 256), bf16),
            pltpu.VMEM((1, 256), bf16),
            pltpu.VMEM((256, 128), f32),
            pltpu.SemaphoreType.DMA((3,)),
        ],
        compiler_params=pltpu.CompilerParams(vmem_limit_bytes=63000000),
    )(projection, phase_shift, direction)
    along = [swap(pack, z_lo, s) for s in (1, 2, 3)]
    other_samples = swap(samples, core, 1)
    ids = (lax.axis_index(RING_X).astype(jnp.int32).reshape(1),)
    work = 2 * 2 * 1024 * 256 * 128 * 10
    acc_of, rows_of = struct((128, 1024)), struct((128, 1024), bf16)
    feats_of = struct((256, 1024), bf16)
    part, low_part = struct((256, 128)), struct((3, 256, 256), bf16)
    firsts = [feats_of, acc_of, rows_of]
    own_first, own_acc, own_rows = call(first_features, firsts, samples, pack, flops=work, ids=ids)
    their_first, their_acc, their_rows = call(
        first_features, firsts, other_samples, pack, flops=work, ids=ids
    )
    their_near, their_acc = call(
        their_near_features,
        [feats_of, acc_of],
        their_rows,
        their_acc,
        along[0],
        after=own_acc,
        flops=work,
    )
    their_far, their_sums = call(
        their_far_features,
        [struct((2, 256, 1024), bf16), struct((1024, 128))],
        their_rows,
        their_acc,
        *along[1:],
        scratch=[pltpu.VMEM((128, 1024), f32)],
        flops=2 * work,
    )
    from_other = swap(their_sums, core, 1)
    own_rest, sums, last = [None] * 4, [None] * 4, their_sums
    for q in (2, 1, 3, 0):
        own_rest[q], sums[q] = call(
            functools.partial(own_quarter, q),
            [low_part, part],
            own_rows,
            own_acc,
            *along,
            *(() if q == 2 else (from_other,)),
            after=last,
            scratch=[pltpu.VMEM((128, 256), f32)],
            flops=3 * work // 4,
        )
        last = sums[q]
        if q == 2:
            last = sums[q] = call(functools.partial(add_quarter, q), part, sums[q], from_other)
        if q:
            sums[q] = swap(sums[q], RING_X, q)
    pieces = exchange(call(four_sum, struct((16, 32, 128)), *sums), RING_Y + ("zhi",))
    low = call(low_copies_kernel, struct((32, 32, 128), bf16), pieces)
    low = exchange(low, RING_X + RING_Y).reshape(4, 256, 128)
    other_low = swap(low, core, 1)
    parts = call(own_back, [part] * 4, own_first, *own_rest, low, flops=work // 5, ids=ids)
    far_parts = call(
        their_far_back, [part] * 2, their_far, other_low, *parts[2:], flops=work // 10, ids=ids
    )
    parts = call(
        their_near_back,
        [part] * 2,
        their_first,
        their_near,
        other_low,
        *parts[:2],
        after=far_parts[1],
        flops=work // 10,
        ids=ids,
    )
    parts = [*parts, *far_parts]
    received = [swap(parts[s], z_lo, s) for s in (1, 2, 3)]
    far_sum = call(two_sum, part, received[1], received[2])
    applied, gram = call(
        gram_kernel, [struct((256, 128)), struct((GRAM, 128))], far_sum, parts[0], received[0], direction, residual
    )
    plane, column = RING_X + RING_Y, RING_Z + ("core",)
    chunk = GRAM // 32
    piece = exchange(gram.reshape(32, chunk, 128), plane)
    piece = exchange(call(sum_copies_kernel, struct((16, chunk, 128)), piece), column)
    piece = exchange(call(sum_copies_kernel, struct((32, chunk, 128)), piece), plane)
    return call(
        final_kernel,
        [struct((256, 128))] * 3,
        piece.reshape(GRAM, 128),
        applied,
        direction,
        residual,
        solution,
    )


def solution(mesh):
    fine = Mesh(mesh.devices.reshape((2,) * 9), AXES)
    rows, cols, state = P(DP, None), P(None, AXES), P(AXES, None)
    return jax.shard_map(
        local,
        mesh=fine,
        in_specs=(rows, cols, cols, state, state, state),
        out_specs=(state, state, state),
        check_vma=False,
    )
```

```python
import functools
import math

import jax
import jax.numpy as jnp
from jax import lax
from jax.experimental import pallas as pl
from jax.experimental.pallas import tpu as pltpu
from jax.sharding import Mesh, PartitionSpec as P

FEATURES = 131072
penalty = 0.1
highest = lax.Precision.HIGHEST
f32 = jnp.float32
bf16 = jnp.bfloat16

SINE = (6.283164044300415, -41.33714237083587, 81.34076887919463, -70.99343319457358)
SCALE = math.sqrt(2.0 / FEATURES)
ROUNDER = 12582912.0
PACK = 272
GRAM = 384

AXES = ("z2", "z1", "core", "y4", "y2", "y1", "x2", "x1", "zhi")
DP = ("z2", "z1", "core")
RING_X = ("x2", "x1")
RING_Y = ("y4", "y2", "y1")
RING_Z = ("zhi", "z2", "z1")


def vmem():
    return pl.BlockSpec(memory_space=pltpu.VMEM)


def call(kernel, outs, *args, scratch=(), flops=0, ids=(), after=None):
    args = (*ids, *args)
    specs = [pl.BlockSpec(memory_space=pltpu.SMEM)] * len(ids) + [vmem()] * (len(args) - len(ids))
    if after is not None:
        args, specs = (*args, after), [*specs, pl.BlockSpec(memory_space=pl.ANY)]
    return pl.pallas_call(
        kernel,
        out_shape=outs,
        in_specs=specs,
        out_specs=jax.tree.map(lambda _: vmem(), outs),
        scratch_shapes=list(scratch),
        compiler_params=pltpu.CompilerParams(vmem_limit_bytes=16 * 1024 * 1024),
        cost_estimate=pl.CostEstimate(flops=flops, bytes_accessed=0, transcendentals=0),
    )(*args)


def struct(shape, dtype=f32):
    return jax.ShapeDtypeStruct(shape, dtype)


def pack_kernel(proj_in, shift_in, dir_in, out_ref, proj_ref, shift_ref, dir_ref, sems):
    copies = [
        pltpu.make_async_copy(src, dst, sems.at[i])
        for i, (src, dst) in enumerate(
            ((dir_in, dir_ref), (proj_in, proj_ref), (shift_in, shift_ref))
        )
    ]
    for c in copies:
        c.start()
    for c in copies:
        c.wait()
    proj_t = proj_ref[...].astype(f32).T.astype(bf16)
    out_ref[0:128, 0:128] = proj_t[0:128]
    out_ref[0:128, 128:256] = proj_t[128:256]
    out_ref[128:144, :] = jnp.broadcast_to(shift_ref[...].astype(f32), (16, 256)).astype(bf16)
    out_ref[144:272, :] = dir_ref[...].T.astype(bf16)


def scaled_cos(phase):
    turns = phase * (1.0 / (2.0 * math.pi))
    turns = turns - ((turns + ROUNDER) - ROUNDER)
    w = 0.25 - jnp.abs(turns)
    z = w * w
    acc = SINE[3] * SCALE
    for c in (SINE[2], SINE[1], SINE[0]):
        acc = acc * z + c * SCALE
    return acc * w


def feature_step(rows_t, piece, feats_ref, acc, quarters, base):
    proj_t = jnp.concatenate([piece[0:128, 0:128], piece[0:128, 128:256]], axis=0)
    shift = piece[128:144, :].astype(f32).T[:, 0:1]
    dir_t = piece[144:272, :]
    for q in quarters:
        rows = slice(q * 256, (q + 1) * 256)
        cols = slice((q - base) * 256, (q - base + 1) * 256)
        phase = jnp.dot(proj_t, rows_t[:, rows], preferred_element_type=f32)
        for i in range(0, 256, 32):
            strip = phase[i : i + 32] + shift[i : i + 32]
            feats_ref[i : i + 32, cols] = scaled_cos(strip).astype(bf16)
        acc[:, cols] += jnp.dot(dir_t, feats_ref[:, cols], preferred_element_type=f32)


def first_features(ids_ref, samples_ref, pack_ref, feats_ref, acc, rows_t):
    for q in range(4):
        start = pl.multiple_of((ids_ref[0] ^ q) * 256, 256)
        rows_t[:, q * 256 : (q + 1) * 256] = samples_ref[pl.ds(start, 256), :].T
    acc[...] = jnp.zeros_like(acc)
    feature_step(rows_t, pack_ref, feats_ref, acc, range(4), 0)


def their_near_features(rows_t, acc_in, p1, after_ref, feats_ref, acc):
    acc[...] = acc_in[...]
    feature_step(rows_t, p1, feats_ref, acc, range(4), 0)


def their_far_features(rows_t, acc_in, p2, p3, feats_ref, sums_ref, acc):
    acc[...] = acc_in[...]
    for s, p in enumerate((p2, p3)):
        feature_step(rows_t, p, feats_ref.at[s], acc, range(4), 0)
    sums_ref[...] = acc[...].T


def own_quarter(q, rows_t, acc_in, p1, p2, p3, *refs):
    feats_ref, sums_ref, acc = refs[-3:]
    acc[...] = acc_in[:, q * 256 : (q + 1) * 256]
    for s, p in enumerate((p1, p2, p3)):
        feature_step(rows_t, p, feats_ref.at[s], acc, (q,), q)
    total = acc[...].T
    if len(refs) == 5:
        total = total + refs[0][q * 256 : (q + 1) * 256, :]
    sums_ref[...] = total


def add_quarter(q, own_ref, other_ref, out_ref):
    out_ref[...] = own_ref[...] + other_ref[q * 256 : (q + 1) * 256, :]


def four_sum(a, b, c, d, out_ref):
    total = (a[...] + b[...]) + (c[...] + d[...])
    for y in range(8):
        for z in range(2):
            out_ref[2 * y + z] = total[32 * y : 32 * y + 32]


def total_of(in_ref):
    total = in_ref[0]
    for i in range(1, in_ref.shape[0]):
        total = total + in_ref[i]
    return total


def sum_copies_kernel(in_ref, out_ref):
    total = total_of(in_ref)
    for i in range(out_ref.shape[0]):
        out_ref[i] = total


def low_copies_kernel(in_ref, out_ref):
    low = total_of(in_ref).astype(bf16)
    for i in range(32):
        out_ref[i] = low


def own_back(ids_ref, first_ref, f0, f1, f2, f3, low_ref, *outs):
    quarters = (f0, f1, f2, f3)
    for s in range(4):
        total = jnp.zeros((256, 128), f32)
        for q in range(4):
            feats = first_ref[:, q * 256 : (q + 1) * 256] if s == 0 else quarters[q][s - 1]
            total += jnp.dot(feats, low_ref[ids_ref[0] ^ q], preferred_element_type=f32)
        outs[s][...] = total


def their_far_back(ids_ref, far_ref, low_ref, a2, a3, *outs):
    for s, part in enumerate((a2, a3)):
        total = part[...]
        for q in range(4):
            feats = far_ref[s, :, q * 256 : (q + 1) * 256]
            total += jnp.dot(feats, low_ref[ids_ref[0] ^ q], preferred_element_type=f32)
        outs[s][...] = total


def their_near_back(ids_ref, first_ref, near_ref, low_ref, a0, a1, after_ref, *outs):
    for s, (ref, part) in enumerate(((first_ref, a0), (near_ref, a1))):
        total = part[...]
        for q in range(4):
            feats = ref[:, q * 256 : (q + 1) * 256]
            total += jnp.dot(feats, low_ref[ids_ref[0] ^ q], preferred_element_type=f32)
        outs[s][...] = total


def fdot(a, b):
    return jnp.dot(a, b, precision=highest, preferred_element_type=f32)


def sym(m):
    return 0.5 * (m + m.T)


def places():
    n = 128
    return lax.broadcasted_iota(jnp.int32, (n, n), 0), lax.broadcasted_iota(jnp.int32, (n, n), 1)


def two_sum(a, b, out_ref):
    out_ref[...] = a[...] + b[...]


def gram_kernel(far, own, near, dir_ref, res_ref, applied_ref, gram_ref):
    total = far[...] + (own[...] + near[...])
    applied = total + penalty * dir_ref[...]
    applied_ref[...] = applied
    applied_t = applied.T
    dir_gram = sym(fdot(applied_t, dir_ref[...]))
    applied_gram = fdot(applied_t, applied)
    res_gram = sym(fdot(res_ref[...].T, res_ref[...]))
    at_row, at_col = places()
    diag = jnp.sum(jnp.where(at_row == at_col, applied_gram, 0.0), axis=1, keepdims=True)
    gram_ref[0:128, :] = jnp.where(at_col >= at_row, dir_gram, applied_gram)
    gram_ref[128:256, :] = fdot(applied_t, res_ref[...])
    gram_ref[256:384, :] = jnp.where(
        at_col >= at_row, res_gram, jnp.where(at_col == 0, diag, diag[0:1, 0:1])
    )


def inverse_factors(mats):
    n, w = 128, 8
    lane = lax.broadcasted_iota(jnp.int32, (w, n), 1)
    sub = lax.broadcasted_iota(jnp.int32, (w, n), 0)

    def row(tile, i):
        return jnp.broadcast_to(tile[i : i + 1, :], (w, n))

    def col(tile, i):
        return jnp.broadcast_to(tile[:, i : i + 1], (w, n))

    tiles = [[m[w * i : w * i + w, :] for i in range(n // w)] for m in mats]
    outs = [([], []) for _ in mats]
    for h in range(n // w):
        k = w * h
        inside = (lane >= k) & (lane < k + w)
        for t, (ms, ns) in zip(tiles, outs):
            home = t[h]
            rows = [row(home, i) for i in range(w)]
            p = {(i, j): col(rows[i], k + j) for i in range(w) for j in range(i + 1)}
            r = [jnp.where(inside, jnp.where(lane == k + i, 1.0, 0.0), rows[i]) for i in range(w)]
            inv, low = [], {}
            for j in range(w):
                inv.append(1.0 / p[j, j])
                for i in range(j + 1, w):
                    low[i, j] = p[i, j] * inv[j]
                for i in range(j + 1, w):
                    for m in range(j + 1, i + 1):
                        p[i, m] = p[i, m] - low[i, j] * p[m, j]
                    r[i] = r[i] - low[i, j] * r[j]
            x = [None] * w
            for j in reversed(range(w)):
                x[j] = r[j] * inv[j]
                for i in range(j + 1, w):
                    x[j] = x[j] - low[i, j] * x[i]
            whole = x[0]
            for j in range(1, w):
                whole = jnp.where(sub == j, x[j], whole)
            if h + 1 < n // w:
                right = jnp.where(lane >= k + w, home, 0.0)
                change = lax.dot_general(
                    right, whole, (((0,), (0,)), ((), ())), precision=highest, preferred_element_type=f32
                )
                for i in range(h + 2, n // w):
                    t[i] = jnp.where(inside, 0.0, t[i]) - change[w * i : w * i + w]
                old = t[h + 1]
                new = jnp.where(inside, 0.0, old)
                for j in range(w):
                    new = new - col(old, k + j) * x[j]
                t[h + 1] = new
            ms.append(jnp.where(lane < k, home, jnp.where(lane == sub + k, 1.0, 0.0)))
            ns.append(jnp.where(lane < k + w, whole, 0.0))
    return [(jnp.concatenate(ms, axis=0), jnp.concatenate(ns, axis=0)) for ms, ns in outs]


def final_kernel(gram_ref, applied_ref, dir_ref, res_ref, sol_ref, sol_out, res_out, dir_out):
    at_row, at_col = places()
    first, cross, third = (gram_ref[128 * i : 128 * i + 128, :] for i in range(3))
    first_t, third_t = first.T, third.T
    dir_gram = jnp.where(at_col >= at_row, first, first_t)
    res_gram = jnp.where(at_col >= at_row, third, third_t)
    diag = jnp.where(at_row == 0, third[127:128, 1:2], third[:, 0:1])
    applied_gram = jnp.where(at_col < at_row, first, jnp.where(at_col == at_row, diag, first_t))
    (m_d, n_d), (m_r, n_r) = inverse_factors([dir_gram, res_gram])
    step = fdot(m_d.T, fdot(n_d, res_gram))
    step_t = step.T
    sol_out[...] = sol_ref[...] + fdot(dir_ref[...], step)
    res_next = res_ref[...] - fdot(applied_ref[...], step)
    res_out[...] = res_next
    both = fdot(step_t, cross)
    gram_next = sym(res_gram - both - both.T + fdot(step_t, fdot(applied_gram, step)))
    mix = fdot(m_r.T, fdot(n_r, gram_next))
    dir_out[...] = res_next + fdot(dir_ref[...], mix)


def swap(value, axes, s):
    n = 2 ** len(axes)
    return lax.ppermute(value, axes, [(i, i ^ s) for i in range(n)])


def exchange(value, axes):
    return lax.all_to_all(value, axes, 0, 0)


def local(samples, projection, phase_shift, solution, residual, direction):
    z_lo = ("z2", "z1")
    core = ("core",)
    pack = pl.pallas_call(
        pack_kernel,
        out_shape=struct((PACK, 256), bf16),
        in_specs=[pl.BlockSpec(memory_space=pltpu.HBM)] * 3,
        out_specs=vmem(),
        scratch_shapes=[
            pltpu.VMEM((128, 256), bf16),
            pltpu.VMEM((1, 256), bf16),
            pltpu.VMEM((256, 128), f32),
            pltpu.SemaphoreType.DMA((3,)),
        ],
        compiler_params=pltpu.CompilerParams(vmem_limit_bytes=63000000),
    )(projection, phase_shift, direction)
    along = [swap(pack, z_lo, s) for s in (1, 2, 3)]
    other_samples = swap(samples, core, 1)
    ids = (lax.axis_index(RING_X).astype(jnp.int32).reshape(1),)
    work = 2 * 2 * 1024 * 256 * 128 * 10
    acc_of, rows_of = struct((128, 1024)), struct((128, 1024), bf16)
    feats_of = struct((256, 1024), bf16)
    part, low_part = struct((256, 128)), struct((3, 256, 256), bf16)
    firsts = [feats_of, acc_of, rows_of]
    own_first, own_acc, own_rows = call(first_features, firsts, samples, pack, flops=work, ids=ids)
    their_first, their_acc, their_rows = call(
        first_features, firsts, other_samples, pack, flops=work, ids=ids
    )
    their_near, their_acc = call(
        their_near_features,
        [feats_of, acc_of],
        their_rows,
        their_acc,
        along[0],
        after=own_acc,
        flops=work,
    )
    their_far, their_sums = call(
        their_far_features,
        [struct((2, 256, 1024), bf16), struct((1024, 128))],
        their_rows,
        their_acc,
        *along[1:],
        scratch=[pltpu.VMEM((128, 1024), f32)],
        flops=2 * work,
    )
    from_other = swap(their_sums, core, 1)
    own_rest, sums, last = [None] * 4, [None] * 4, their_sums
    for q in (2, 1, 3, 0):
        own_rest[q], sums[q] = call(
            functools.partial(own_quarter, q),
            [low_part, part],
            own_rows,
            own_acc,
            *along,
            *(() if q == 2 else (from_other,)),
            after=last,
            scratch=[pltpu.VMEM((128, 256), f32)],
            flops=3 * work // 4,
        )
        last = sums[q]
        if q == 2:
            last = sums[q] = call(functools.partial(add_quarter, q), part, sums[q], from_other)
        if q:
            sums[q] = swap(sums[q], RING_X, q)
    pieces = exchange(call(four_sum, struct((16, 32, 128)), *sums), RING_Y + ("zhi",))
    low = call(low_copies_kernel, struct((32, 32, 128), bf16), pieces)
    low = exchange(low, RING_X + RING_Y).reshape(4, 256, 128)
    other_low = swap(low, core, 1)
    parts = call(own_back, [part] * 4, own_first, *own_rest, low, flops=work // 5, ids=ids)
    far_parts = call(
        their_far_back, [part] * 2, their_far, other_low, *parts[2:], flops=work // 10, ids=ids
    )
    parts = call(
        their_near_back,
        [part] * 2,
        their_first,
        their_near,
        other_low,
        *parts[:2],
        after=far_parts[1],
        flops=work // 10,
        ids=ids,
    )
    parts = [*parts, *far_parts]
    received = [swap(parts[s], z_lo, s) for s in (1, 2, 3)]
    far_sum = call(two_sum, part, received[1], received[2])
    applied, gram = call(
        gram_kernel, [struct((256, 128)), struct((GRAM, 128))], far_sum, parts[0], received[0], direction, residual
    )
    near, far = RING_X + ("core", "y1"), ("y4", "y2") + RING_Z
    chunk = GRAM // 16
    piece = exchange(gram.reshape(16, chunk, 128), near)
    piece = exchange(call(sum_copies_kernel, struct((32, chunk, 128)), piece), far)
    piece = exchange(call(sum_copies_kernel, struct((16, chunk, 128)), piece), near)
    return call(
        final_kernel,
        [struct((256, 128))] * 3,
        piece.reshape(GRAM, 128),
        applied,
        direction,
        residual,
        solution,
    )


def solution(mesh):
    fine = Mesh(mesh.devices.reshape((2,) * 9), AXES)
    rows, cols, state = P(DP, None), P(None, AXES), P(AXES, None)
    return jax.shard_map(
        local,
        mesh=fine,
        in_specs=(rows, cols, cols, state, state, state),
        out_specs=(state, state, state),
        check_vma=False,
    )
```

```python
import functools
import math

import jax
import jax.numpy as jnp
from jax import lax
from jax.experimental import pallas as pl
from jax.experimental.pallas import tpu as pltpu
from jax.sharding import Mesh, PartitionSpec as P

FEATURES = 131072
penalty = 0.1
highest = lax.Precision.HIGHEST
f32 = jnp.float32
bf16 = jnp.bfloat16

SINE = (6.283164044300415, -41.33714237083587, 81.34076887919463, -70.99343319457358)
SCALE = math.sqrt(2.0 / FEATURES)
ROUNDER = 12582912.0
PACK = 272
GRAM = 512

AXES = ("z2", "z1", "core", "y4", "y2", "y1", "x2", "x1", "zhi")
DP = ("z2", "z1", "core")
RING_X = ("x2", "x1")
RING_Y = ("y4", "y2", "y1")
RING_Z = ("zhi", "z2", "z1")


def vmem():
    return pl.BlockSpec(memory_space=pltpu.VMEM)


def call(kernel, outs, *args, scratch=(), flops=0, ids=(), after=None):
    args = (*ids, *args)
    specs = [pl.BlockSpec(memory_space=pltpu.SMEM)] * len(ids) + [vmem()] * (len(args) - len(ids))
    if after is not None:
        args, specs = (*args, after), [*specs, pl.BlockSpec(memory_space=pl.ANY)]
    return pl.pallas_call(
        kernel,
        out_shape=outs,
        in_specs=specs,
        out_specs=jax.tree.map(lambda _: vmem(), outs),
        scratch_shapes=list(scratch),
        compiler_params=pltpu.CompilerParams(vmem_limit_bytes=16 * 1024 * 1024),
        cost_estimate=pl.CostEstimate(flops=flops, bytes_accessed=0, transcendentals=0),
    )(*args)


def struct(shape, dtype=f32):
    return jax.ShapeDtypeStruct(shape, dtype)


def pack_kernel(proj_in, shift_in, dir_in, out_ref, proj_ref, shift_ref, dir_ref, sems):
    copies = [
        pltpu.make_async_copy(src, dst, sems.at[i])
        for i, (src, dst) in enumerate(
            ((dir_in, dir_ref), (proj_in, proj_ref), (shift_in, shift_ref))
        )
    ]
    for c in copies:
        c.start()
    for c in copies:
        c.wait()
    proj_t = proj_ref[...].astype(f32).T.astype(bf16)
    out_ref[0:128, 0:128] = proj_t[0:128]
    out_ref[0:128, 128:256] = proj_t[128:256]
    out_ref[128:144, :] = jnp.broadcast_to(shift_ref[...].astype(f32), (16, 256)).astype(bf16)
    out_ref[144:272, :] = dir_ref[...].T.astype(bf16)


def scaled_cos(phase):
    turns = phase * (1.0 / (2.0 * math.pi))
    turns = turns - ((turns + ROUNDER) - ROUNDER)
    w = 0.25 - jnp.abs(turns)
    z = w * w
    acc = SINE[3] * SCALE
    for c in (SINE[2], SINE[1], SINE[0]):
        acc = acc * z + c * SCALE
    return acc * w


def feature_step(rows_t, piece, feats_ref, acc, quarters, base):
    proj_t = jnp.concatenate([piece[0:128, 0:128], piece[0:128, 128:256]], axis=0)
    shift = piece[128:144, :].astype(f32).T[:, 0:1]
    dir_t = piece[144:272, :]
    for q in quarters:
        rows = slice(q * 256, (q + 1) * 256)
        cols = slice((q - base) * 256, (q - base + 1) * 256)
        phase = jnp.dot(proj_t, rows_t[:, rows], preferred_element_type=f32)
        for i in range(0, 256, 32):
            strip = phase[i : i + 32] + shift[i : i + 32]
            feats_ref[i : i + 32, cols] = scaled_cos(strip).astype(bf16)
        acc[:, cols] += jnp.dot(dir_t, feats_ref[:, cols], preferred_element_type=f32)


def first_features(ids_ref, samples_ref, pack_ref, feats_ref, acc, rows_t):
    for q in range(4):
        start = pl.multiple_of((ids_ref[0] ^ q) * 256, 256)
        rows_t[:, q * 256 : (q + 1) * 256] = samples_ref[pl.ds(start, 256), :].T
    acc[...] = jnp.zeros_like(acc)
    feature_step(rows_t, pack_ref, feats_ref, acc, range(4), 0)


def their_near_features(rows_t, acc_in, p1, after_ref, feats_ref, acc):
    acc[...] = acc_in[...]
    feature_step(rows_t, p1, feats_ref, acc, range(4), 0)


def their_far_features(rows_t, acc_in, p2, p3, feats_ref, sums_ref, acc):
    acc[...] = acc_in[...]
    for s, p in enumerate((p2, p3)):
        feature_step(rows_t, p, feats_ref.at[s], acc, range(4), 0)
    sums_ref[...] = acc[...].T


def own_quarter(q, rows_t, acc_in, p1, p2, p3, *refs):
    feats_ref, sums_ref, acc = refs[-3:]
    acc[...] = acc_in[:, q * 256 : (q + 1) * 256]
    for s, p in enumerate((p1, p2, p3)):
        feature_step(rows_t, p, feats_ref.at[s], acc, (q,), q)
    total = acc[...].T
    if len(refs) == 5:
        total = total + refs[0][q * 256 : (q + 1) * 256, :]
    sums_ref[...] = total


def add_quarter(q, own_ref, other_ref, out_ref):
    out_ref[...] = own_ref[...] + other_ref[q * 256 : (q + 1) * 256, :]


def four_sum(a, b, c, d, out_ref):
    total = (a[...] + b[...]) + (c[...] + d[...])
    for y in range(8):
        for z in range(2):
            out_ref[2 * y + z] = total[32 * y : 32 * y + 32]


def total_of(in_ref):
    total = in_ref[0]
    for i in range(1, in_ref.shape[0]):
        total = total + in_ref[i]
    return total


def sum_copies_kernel(in_ref, out_ref):
    total = total_of(in_ref)
    for i in range(out_ref.shape[0]):
        out_ref[i] = total


def low_copies_kernel(in_ref, out_ref):
    low = total_of(in_ref).astype(bf16)
    for i in range(32):
        out_ref[i] = low


def own_back(ids_ref, first_ref, f0, f1, f2, f3, low_ref, *outs):
    quarters = (f0, f1, f2, f3)
    for s in range(4):
        total = jnp.zeros((256, 128), f32)
        for q in range(4):
            feats = first_ref[:, q * 256 : (q + 1) * 256] if s == 0 else quarters[q][s - 1]
            total += jnp.dot(feats, low_ref[ids_ref[0] ^ q], preferred_element_type=f32)
        outs[s][...] = total


def their_far_back(ids_ref, far_ref, low_ref, a2, a3, *outs):
    for s, part in enumerate((a2, a3)):
        total = part[...]
        for q in range(4):
            feats = far_ref[s, :, q * 256 : (q + 1) * 256]
            total += jnp.dot(feats, low_ref[ids_ref[0] ^ q], preferred_element_type=f32)
        outs[s][...] = total


def their_near_back(ids_ref, first_ref, near_ref, low_ref, a0, a1, after_ref, *outs):
    for s, (ref, part) in enumerate(((first_ref, a0), (near_ref, a1))):
        total = part[...]
        for q in range(4):
            feats = ref[:, q * 256 : (q + 1) * 256]
            total += jnp.dot(feats, low_ref[ids_ref[0] ^ q], preferred_element_type=f32)
        outs[s][...] = total


def fdot(a, b):
    return jnp.dot(a, b, precision=highest, preferred_element_type=f32)


def sym(m):
    return 0.5 * (m + m.T)


def two_sum(a, b, out_ref):
    out_ref[...] = a[...] + b[...]


def gram_kernel(far, own, near, dir_ref, res_ref, applied_ref, gram_ref):
    total = far[...] + (own[...] + near[...])
    applied = total + penalty * dir_ref[...]
    applied_ref[...] = applied
    applied_t = applied.T
    grams = (
        fdot(applied_t, dir_ref[...]),
        fdot(applied_t, res_ref[...]),
        fdot(applied_t, applied),
        fdot(res_ref[...].T, res_ref[...]),
    )
    for i, g in enumerate(grams):
        gram_ref[128 * i : 128 * i + 128, :] = g


def inverse_factors(mats):
    n, w = 128, 8
    lane = lax.broadcasted_iota(jnp.int32, (w, n), 1)
    sub = lax.broadcasted_iota(jnp.int32, (w, n), 0)

    def row(tile, i):
        return jnp.broadcast_to(tile[i : i + 1, :], (w, n))

    def col(tile, i):
        return jnp.broadcast_to(tile[:, i : i + 1], (w, n))

    tiles = [[m[w * i : w * i + w, :] for i in range(n // w)] for m in mats]
    outs = [([], []) for _ in mats]
    for h in range(n // w):
        k = w * h
        inside = (lane >= k) & (lane < k + w)
        for t, (ms, ns) in zip(tiles, outs):
            home = t[h]
            rows = [row(home, i) for i in range(w)]
            p = {(i, j): col(rows[i], k + j) for i in range(w) for j in range(i + 1)}
            r = [jnp.where(inside, jnp.where(lane == k + i, 1.0, 0.0), rows[i]) for i in range(w)]
            inv, low = [], {}
            for j in range(w):
                inv.append(1.0 / p[j, j])
                for i in range(j + 1, w):
                    low[i, j] = p[i, j] * inv[j]
                for i in range(j + 1, w):
                    for m in range(j + 1, i + 1):
                        p[i, m] = p[i, m] - low[i, j] * p[m, j]
                    r[i] = r[i] - low[i, j] * r[j]
            x = [None] * w
            for j in reversed(range(w)):
                x[j] = r[j] * inv[j]
                for i in range(j + 1, w):
                    x[j] = x[j] - low[i, j] * x[i]
            whole = x[0]
            for j in range(1, w):
                whole = jnp.where(sub == j, x[j], whole)
            if h + 1 < n // w:
                right = jnp.where(lane >= k + w, home, 0.0)
                change = lax.dot_general(
                    right, whole, (((0,), (0,)), ((), ())), precision=highest, preferred_element_type=f32
                )
                for i in range(h + 2, n // w):
                    t[i] = jnp.where(inside, 0.0, t[i]) - change[w * i : w * i + w]
                old = t[h + 1]
                new = jnp.where(inside, 0.0, old)
                for j in range(w):
                    new = new - col(old, k + j) * x[j]
                t[h + 1] = new
            ms.append(jnp.where(lane < k, home, jnp.where(lane == sub + k, 1.0, 0.0)))
            ns.append(jnp.where(lane < k + w, whole, 0.0))
    return [(jnp.concatenate(ms, axis=0), jnp.concatenate(ns, axis=0)) for ms, ns in outs]


def final_kernel(gram_ref, applied_ref, dir_ref, res_ref, sol_ref, sol_out, res_out, dir_out):
    dir_gram = sym(gram_ref[0:128, :])
    cross = gram_ref[128:256, :]
    applied_gram = gram_ref[256:384, :]
    res_gram = sym(gram_ref[384:512, :])
    (m_d, n_d), (m_r, n_r) = inverse_factors([dir_gram, res_gram])
    step = fdot(m_d.T, fdot(n_d, res_gram))
    step_t = step.T
    sol_out[...] = sol_ref[...] + fdot(dir_ref[...], step)
    res_next = res_ref[...] - fdot(applied_ref[...], step)
    res_out[...] = res_next
    both = fdot(step_t, cross)
    gram_next = sym(res_gram - both - both.T + fdot(step_t, fdot(applied_gram, step)))
    mix = fdot(m_r.T, fdot(n_r, gram_next))
    dir_out[...] = res_next + fdot(dir_ref[...], mix)


def swap(value, axes, s):
    n = 2 ** len(axes)
    return lax.ppermute(value, axes, [(i, i ^ s) for i in range(n)])


def exchange(value, axes):
    return lax.all_to_all(value, axes, 0, 0)


def local(samples, projection, phase_shift, solution, residual, direction):
    z_lo = ("z2", "z1")
    core = ("core",)
    pack = pl.pallas_call(
        pack_kernel,
        out_shape=struct((PACK, 256), bf16),
        in_specs=[pl.BlockSpec(memory_space=pltpu.HBM)] * 3,
        out_specs=vmem(),
        scratch_shapes=[
            pltpu.VMEM((128, 256), bf16),
            pltpu.VMEM((1, 256), bf16),
            pltpu.VMEM((256, 128), f32),
            pltpu.SemaphoreType.DMA((3,)),
        ],
        compiler_params=pltpu.CompilerParams(vmem_limit_bytes=63000000),
    )(projection, phase_shift, direction)
    along = [swap(pack, z_lo, s) for s in (1, 2, 3)]
    other_samples = swap(samples, core, 1)
    ids = (lax.axis_index(RING_X).astype(jnp.int32).reshape(1),)
    work = 2 * 2 * 1024 * 256 * 128 * 10
    acc_of, rows_of = struct((128, 1024)), struct((128, 1024), bf16)
    feats_of = struct((256, 1024), bf16)
    part, low_part = struct((256, 128)), struct((3, 256, 256), bf16)
    firsts = [feats_of, acc_of, rows_of]
    own_first, own_acc, own_rows = call(first_features, firsts, samples, pack, flops=work, ids=ids)
    their_first, their_acc, their_rows = call(
        first_features, firsts, other_samples, pack, flops=work, ids=ids
    )
    their_near, their_acc = call(
        their_near_features,
        [feats_of, acc_of],
        their_rows,
        their_acc,
        along[0],
        after=own_acc,
        flops=work,
    )
    their_far, their_sums = call(
        their_far_features,
        [struct((2, 256, 1024), bf16), struct((1024, 128))],
        their_rows,
        their_acc,
        *along[1:],
        scratch=[pltpu.VMEM((128, 1024), f32)],
        flops=2 * work,
    )
    from_other = swap(their_sums, core, 1)
    own_rest, sums, last = [None] * 4, [None] * 4, their_sums
    for q in (2, 1, 3, 0):
        own_rest[q], sums[q] = call(
            functools.partial(own_quarter, q),
            [low_part, part],
            own_rows,
            own_acc,
            *along,
            *(() if q == 2 else (from_other,)),
            after=last,
            scratch=[pltpu.VMEM((128, 256), f32)],
            flops=3 * work // 4,
        )
        last = sums[q]
        if q == 2:
            last = sums[q] = call(functools.partial(add_quarter, q), part, sums[q], from_other)
        if q:
            sums[q] = swap(sums[q], RING_X, q)
    pieces = exchange(call(four_sum, struct((16, 32, 128)), *sums), RING_Y + ("zhi",))
    low = call(low_copies_kernel, struct((32, 32, 128), bf16), pieces)
    low = exchange(low, RING_X + RING_Y).reshape(4, 256, 128)
    other_low = swap(low, core, 1)
    parts = call(own_back, [part] * 4, own_first, *own_rest, low, flops=work // 5, ids=ids)
    far_parts = call(
        their_far_back, [part] * 2, their_far, other_low, *parts[2:], flops=work // 10, ids=ids
    )
    parts = call(
        their_near_back,
        [part] * 2,
        their_first,
        their_near,
        other_low,
        *parts[:2],
        after=far_parts[1],
        flops=work // 10,
        ids=ids,
    )
    parts = [*parts, *far_parts]
    received = [swap(parts[s], z_lo, s) for s in (1, 2, 3)]
    far_sum = call(two_sum, part, received[1], received[2])
    applied, gram = call(
        gram_kernel, [struct((256, 128)), struct((GRAM, 128))], far_sum, parts[0], received[0], direction, residual
    )
    plane, column = RING_X + ("core", "y1", "z1"), ("y4", "y2", "zhi", "z2")
    chunk = GRAM // 32
    piece = exchange(gram.reshape(32, chunk, 128), plane)
    piece = exchange(call(sum_copies_kernel, struct((16, chunk, 128)), piece), column)
    piece = exchange(call(sum_copies_kernel, struct((32, chunk, 128)), piece), plane)
    return call(
        final_kernel,
        [struct((256, 128))] * 3,
        piece.reshape(GRAM, 128),
        applied,
        direction,
        residual,
        solution,
    )


def solution(mesh):
    fine = Mesh(mesh.devices.reshape((2,) * 9), AXES)
    rows, cols, state = P(DP, None), P(None, AXES), P(AXES, None)
    return jax.shard_map(
        local,
        mesh=fine,
        in_specs=(rows, cols, cols, state, state, state),
        out_specs=(state, state, state),
        check_vma=False,
    )
```

```python
import functools
import math

import jax
import jax.numpy as jnp
from jax import lax
from jax.experimental import pallas as pl
from jax.experimental.pallas import tpu as pltpu
from jax.sharding import Mesh, PartitionSpec as P

FEATURES = 131072
penalty = 0.1
highest = lax.Precision.HIGHEST
f32 = jnp.float32
bf16 = jnp.bfloat16

SINE = (6.283164044300415, -41.33714237083587, 81.34076887919463, -70.99343319457358)
SCALE = math.sqrt(2.0 / FEATURES)
ROUNDER = 12582912.0
PACK = 272
GRAM = 512

AXES = ("z2", "z1", "core", "y4", "y2", "y1", "x2", "x1", "zhi")
DP = ("z2", "z1", "core")
RING_X = ("x2", "x1")
RING_Y = ("y4", "y2", "y1")
RING_Z = ("zhi", "z2", "z1")


def vmem():
    return pl.BlockSpec(memory_space=pltpu.VMEM)


def call(kernel, outs, *args, scratch=(), flops=0, ids=(), after=None):
    args = (*ids, *args)
    specs = [pl.BlockSpec(memory_space=pltpu.SMEM)] * len(ids) + [vmem()] * (len(args) - len(ids))
    if after is not None:
        args, specs = (*args, after), [*specs, pl.BlockSpec(memory_space=pl.ANY)]
    return pl.pallas_call(
        kernel,
        out_shape=outs,
        in_specs=specs,
        out_specs=jax.tree.map(lambda _: vmem(), outs),
        scratch_shapes=list(scratch),
        compiler_params=pltpu.CompilerParams(vmem_limit_bytes=16 * 1024 * 1024),
        cost_estimate=pl.CostEstimate(flops=flops, bytes_accessed=0, transcendentals=0),
    )(*args)


def struct(shape, dtype=f32):
    return jax.ShapeDtypeStruct(shape, dtype)


def pack_kernel(proj_in, shift_in, dir_in, out_ref, proj_ref, shift_ref, dir_ref, sems):
    copies = [
        pltpu.make_async_copy(src, dst, sems.at[i])
        for i, (src, dst) in enumerate(
            ((dir_in, dir_ref), (proj_in, proj_ref), (shift_in, shift_ref))
        )
    ]
    for c in copies:
        c.start()
    for c in copies:
        c.wait()
    proj_t = proj_ref[...].astype(f32).T.astype(bf16)
    out_ref[0:128, 0:128] = proj_t[0:128]
    out_ref[0:128, 128:256] = proj_t[128:256]
    out_ref[128:144, :] = jnp.broadcast_to(shift_ref[...].astype(f32), (16, 256)).astype(bf16)
    out_ref[144:272, :] = dir_ref[...].T.astype(bf16)


def scaled_cos(phase):
    turns = phase * (1.0 / (2.0 * math.pi))
    turns = turns - ((turns + ROUNDER) - ROUNDER)
    w = 0.25 - jnp.abs(turns)
    z = w * w
    acc = SINE[3] * SCALE
    for c in (SINE[2], SINE[1], SINE[0]):
        acc = acc * z + c * SCALE
    return acc * w


def feature_step(rows_t, piece, feats_ref, acc, quarters, base):
    proj_t = jnp.concatenate([piece[0:128, 0:128], piece[0:128, 128:256]], axis=0)
    shift = piece[128:144, :].astype(f32).T[:, 0:1]
    dir_t = piece[144:272, :]
    for q in quarters:
        rows = slice(q * 256, (q + 1) * 256)
        cols = slice((q - base) * 256, (q - base + 1) * 256)
        phase = jnp.dot(proj_t, rows_t[:, rows], preferred_element_type=f32)
        for i in range(0, 256, 32):
            strip = phase[i : i + 32] + shift[i : i + 32]
            feats_ref[i : i + 32, cols] = scaled_cos(strip).astype(bf16)
        acc[:, cols] += jnp.dot(dir_t, feats_ref[:, cols], preferred_element_type=f32)


def first_features(ids_ref, samples_ref, pack_ref, feats_ref, acc, rows_t):
    for q in range(4):
        start = pl.multiple_of((ids_ref[0] ^ q) * 256, 256)
        rows_t[:, q * 256 : (q + 1) * 256] = samples_ref[pl.ds(start, 256), :].T
    acc[...] = jnp.zeros_like(acc)
    feature_step(rows_t, pack_ref, feats_ref, acc, range(4), 0)


def their_near_features(rows_t, acc_in, p1, after_ref, feats_ref, acc):
    acc[...] = acc_in[...]
    feature_step(rows_t, p1, feats_ref, acc, range(4), 0)


def their_far_features(rows_t, acc_in, p2, p3, feats_ref, sums_ref, acc):
    acc[...] = acc_in[...]
    for s, p in enumerate((p2, p3)):
        feature_step(rows_t, p, feats_ref.at[s], acc, range(4), 0)
    sums_ref[...] = acc[...].T


def own_quarter(q, rows_t, acc_in, p1, p2, p3, *refs):
    feats_ref, sums_ref, acc = refs[-3:]
    acc[...] = acc_in[:, q * 256 : (q + 1) * 256]
    for s, p in enumerate((p1, p2, p3)):
        feature_step(rows_t, p, feats_ref.at[s], acc, (q,), q)
    total = acc[...].T
    if len(refs) == 5:
        total = total + refs[0][q * 256 : (q + 1) * 256, :]
    sums_ref[...] = total


def add_quarter(q, own_ref, other_ref, out_ref):
    out_ref[...] = own_ref[...] + other_ref[q * 256 : (q + 1) * 256, :]


def four_sum(a, b, c, d, out_ref):
    total = (a[...] + b[...]) + (c[...] + d[...])
    for y in range(8):
        for z in range(2):
            out_ref[2 * y + z] = total[32 * y : 32 * y + 32]


def total_of(in_ref):
    total = in_ref[0]
    for i in range(1, in_ref.shape[0]):
        total = total + in_ref[i]
    return total


def sum_copies_kernel(in_ref, out_ref):
    total = total_of(in_ref)
    for i in range(out_ref.shape[0]):
        out_ref[i] = total


def low_copies_kernel(in_ref, out_ref):
    low = total_of(in_ref).astype(bf16)
    for i in range(32):
        out_ref[i] = low


def own_back(ids_ref, first_ref, f0, f1, f2, f3, low_ref, *outs):
    quarters = (f0, f1, f2, f3)
    for s in range(4):
        total = jnp.zeros((256, 128), f32)
        for q in range(4):
            feats = first_ref[:, q * 256 : (q + 1) * 256] if s == 0 else quarters[q][s - 1]
            total += jnp.dot(feats, low_ref[ids_ref[0] ^ q], preferred_element_type=f32)
        outs[s][...] = total


def their_far_back(ids_ref, far_ref, low_ref, a2, a3, *outs):
    for s, part in enumerate((a2, a3)):
        total = part[...]
        for q in range(4):
            feats = far_ref[s, :, q * 256 : (q + 1) * 256]
            total += jnp.dot(feats, low_ref[ids_ref[0] ^ q], preferred_element_type=f32)
        outs[s][...] = total


def their_near_back(ids_ref, first_ref, near_ref, low_ref, a0, a1, after_ref, *outs):
    for s, (ref, part) in enumerate(((first_ref, a0), (near_ref, a1))):
        total = part[...]
        for q in range(4):
            feats = ref[:, q * 256 : (q + 1) * 256]
            total += jnp.dot(feats, low_ref[ids_ref[0] ^ q], preferred_element_type=f32)
        outs[s][...] = total


def fdot(a, b):
    return jnp.dot(a, b, precision=highest, preferred_element_type=f32)


def sym(m):
    return 0.5 * (m + m.T)


def two_sum(a, b, out_ref):
    out_ref[...] = a[...] + b[...]


def gram_kernel(far, own, near, dir_ref, res_ref, applied_ref, gram_ref):
    total = far[...] + (own[...] + near[...])
    applied = total + penalty * dir_ref[...]
    applied_ref[...] = applied
    applied_t = applied.T
    grams = (
        fdot(applied_t, dir_ref[...]),
        fdot(applied_t, res_ref[...]),
        fdot(applied_t, applied),
        fdot(res_ref[...].T, res_ref[...]),
    )
    for i, g in enumerate(grams):
        gram_ref[128 * i : 128 * i + 128, :] = g


def inverse_factors(mats):
    n, w = 128, 8
    lane = lax.broadcasted_iota(jnp.int32, (w, n), 1)
    sub = lax.broadcasted_iota(jnp.int32, (w, n), 0)

    def row(tile, i):
        return jnp.broadcast_to(tile[i : i + 1, :], (w, n))

    def col(tile, i):
        return jnp.broadcast_to(tile[:, i : i + 1], (w, n))

    tiles = [[m[w * i : w * i + w, :] for i in range(n // w)] for m in mats]
    outs = [([], []) for _ in mats]
    for h in range(n // w):
        k = w * h
        inside = (lane >= k) & (lane < k + w)
        for t, (ms, ns) in zip(tiles, outs):
            home = t[h]
            rows = [row(home, i) for i in range(w)]
            p = {(i, j): col(rows[i], k + j) for i in range(w) for j in range(i + 1)}
            r = [jnp.where(inside, jnp.where(lane == k + i, 1.0, 0.0), rows[i]) for i in range(w)]
            inv, low = [], {}
            for j in range(w):
                inv.append(pl.reciprocal(p[j, j], approx=False))
                for i in range(j + 1, w):
                    low[i, j] = p[i, j] * inv[j]
                for i in range(j + 1, w):
                    for m in range(j + 1, i + 1):
                        p[i, m] = p[i, m] - low[i, j] * p[m, j]
                    r[i] = r[i] - low[i, j] * r[j]
            x = [None] * w
            for j in reversed(range(w)):
                x[j] = r[j] * inv[j]
                for i in range(j + 1, w):
                    x[j] = x[j] - low[i, j] * x[i]
            whole = x[0]
            for j in range(1, w):
                whole = jnp.where(sub == j, x[j], whole)
            if h + 1 < n // w:
                right = jnp.where(lane >= k + w, home, 0.0)
                change = lax.dot_general(
                    right, whole, (((0,), (0,)), ((), ())), precision=highest, preferred_element_type=f32
                )
                for i in range(h + 2, n // w):
                    t[i] = jnp.where(inside, 0.0, t[i]) - change[w * i : w * i + w]
                old = t[h + 1]
                new = jnp.where(inside, 0.0, old)
                for j in range(w):
                    new = new - col(old, k + j) * x[j]
                t[h + 1] = new
            ms.append(jnp.where(lane < k, home, jnp.where(lane == sub + k, 1.0, 0.0)))
            ns.append(jnp.where(lane < k + w, whole, 0.0))
    return [(jnp.concatenate(ms, axis=0), jnp.concatenate(ns, axis=0)) for ms, ns in outs]


def final_kernel(gram_ref, applied_ref, dir_ref, res_ref, sol_ref, sol_out, res_out, dir_out):
    dir_gram = sym(gram_ref[0:128, :])
    cross = gram_ref[128:256, :]
    applied_gram = gram_ref[256:384, :]
    res_gram = sym(gram_ref[384:512, :])
    (m_d, n_d), (m_r, n_r) = inverse_factors([dir_gram, res_gram])
    step = fdot(m_d.T, fdot(n_d, res_gram))
    step_t = step.T
    sol_out[...] = sol_ref[...] + fdot(dir_ref[...], step)
    res_next = res_ref[...] - fdot(applied_ref[...], step)
    res_out[...] = res_next
    both = fdot(step_t, cross)
    gram_next = sym(res_gram - both - both.T + fdot(step_t, fdot(applied_gram, step)))
    mix = fdot(m_r.T, fdot(n_r, gram_next))
    dir_out[...] = res_next + fdot(dir_ref[...], mix)


def swap(value, axes, s):
    n = 2 ** len(axes)
    return lax.ppermute(value, axes, [(i, i ^ s) for i in range(n)])


def exchange(value, axes):
    return lax.all_to_all(value, axes, 0, 0)


def local(samples, projection, phase_shift, solution, residual, direction):
    z_lo = ("z2", "z1")
    core = ("core",)
    pack = pl.pallas_call(
        pack_kernel,
        out_shape=struct((PACK, 256), bf16),
        in_specs=[pl.BlockSpec(memory_space=pltpu.HBM)] * 3,
        out_specs=vmem(),
        scratch_shapes=[
            pltpu.VMEM((128, 256), bf16),
            pltpu.VMEM((1, 256), bf16),
            pltpu.VMEM((256, 128), f32),
            pltpu.SemaphoreType.DMA((3,)),
        ],
        compiler_params=pltpu.CompilerParams(vmem_limit_bytes=63000000),
    )(projection, phase_shift, direction)
    along = [swap(pack, z_lo, s) for s in (1, 2, 3)]
    other_samples = swap(samples, core, 1)
    ids = (lax.axis_index(RING_X).astype(jnp.int32).reshape(1),)
    work = 2 * 2 * 1024 * 256 * 128 * 10
    acc_of, rows_of = struct((128, 1024)), struct((128, 1024), bf16)
    feats_of = struct((256, 1024), bf16)
    part, low_part = struct((256, 128)), struct((3, 256, 256), bf16)
    firsts = [feats_of, acc_of, rows_of]
    own_first, own_acc, own_rows = call(first_features, firsts, samples, pack, flops=work, ids=ids)
    their_first, their_acc, their_rows = call(
        first_features, firsts, other_samples, pack, flops=work, ids=ids
    )
    their_near, their_acc = call(
        their_near_features,
        [feats_of, acc_of],
        their_rows,
        their_acc,
        along[0],
        after=own_acc,
        flops=work,
    )
    their_far, their_sums = call(
        their_far_features,
        [struct((2, 256, 1024), bf16), struct((1024, 128))],
        their_rows,
        their_acc,
        *along[1:],
        scratch=[pltpu.VMEM((128, 1024), f32)],
        flops=2 * work,
    )
    from_other = swap(their_sums, core, 1)
    own_rest, sums, last = [None] * 4, [None] * 4, their_sums
    for q in (2, 1, 3, 0):
        own_rest[q], sums[q] = call(
            functools.partial(own_quarter, q),
            [low_part, part],
            own_rows,
            own_acc,
            *along,
            *(() if q == 2 else (from_other,)),
            after=last,
            scratch=[pltpu.VMEM((128, 256), f32)],
            flops=3 * work // 4,
        )
        last = sums[q]
        if q == 2:
            last = sums[q] = call(functools.partial(add_quarter, q), part, sums[q], from_other)
        if q:
            sums[q] = swap(sums[q], RING_X, q)
    pieces = exchange(call(four_sum, struct((16, 32, 128)), *sums), RING_Y + ("zhi",))
    low = call(low_copies_kernel, struct((32, 32, 128), bf16), pieces)
    low = exchange(low, RING_X + RING_Y).reshape(4, 256, 128)
    other_low = swap(low, core, 1)
    parts = call(own_back, [part] * 4, own_first, *own_rest, low, flops=work // 5, ids=ids)
    far_parts = call(
        their_far_back, [part] * 2, their_far, other_low, *parts[2:], flops=work // 10, ids=ids
    )
    parts = call(
        their_near_back,
        [part] * 2,
        their_first,
        their_near,
        other_low,
        *parts[:2],
        after=far_parts[1],
        flops=work // 10,
        ids=ids,
    )
    parts = [*parts, *far_parts]
    received = [swap(parts[s], z_lo, s) for s in (1, 2, 3)]
    far_sum = call(two_sum, part, received[1], received[2])
    applied, gram = call(
        gram_kernel, [struct((256, 128)), struct((GRAM, 128))], far_sum, parts[0], received[0], direction, residual
    )
    plane, column = RING_X + ("core", "y1", "z1"), ("y4", "y2", "zhi", "z2")
    chunk = GRAM // 32
    piece = exchange(gram.reshape(32, chunk, 128), plane)
    piece = exchange(call(sum_copies_kernel, struct((16, chunk, 128)), piece), column)
    piece = exchange(call(sum_copies_kernel, struct((32, chunk, 128)), piece), plane)
    return call(
        final_kernel,
        [struct((256, 128))] * 3,
        piece.reshape(GRAM, 128),
        applied,
        direction,
        residual,
        solution,
    )


def solution(mesh):
    fine = Mesh(mesh.devices.reshape((2,) * 9), AXES)
    rows, cols, state = P(DP, None), P(None, AXES), P(AXES, None)
    return jax.shard_map(
        local,
        mesh=fine,
        in_specs=(rows, cols, cols, state, state, state),
        out_specs=(state, state, state),
        check_vma=False,
    )
```
